1024 devices in a mesh: blk: 32 (over z, x_hi), grp: 32 (over x_lo, y, core).
Axes of the slice: x: 4 (x_hi: 2, x_lo: 2; x = x_hi * 2 + x_lo), y: 8, z: 16, core: 2. Of those that a mesh axis runs over, the one named last changes fastest.
Arguments:
- counts: bfloat16 [4, 32768, 8192], P(None, 'blk', 'grp'), may hold values from 0 to 200
- row_sums: int32 [32768], P('blk'), may hold values from 1000 to 29999
- col_sums: int32 [262144], P(('blk', 'grp')), may hold values from 1000 to 29999
- row_emb: float32 [300, 32768], P(None, 'blk'), may hold values from -1.5 to 1.5
- row_acc: float32 [300, 32768], P(None, 'blk'), may hold values from 0.05 to 0.5
- col_emb: float32 [300, 262144], P(None, ('blk', 'grp')), may hold values from -1.5 to 1.5
- col_acc: float32 [300, 262144], P(None, ('blk', 'grp')), may hold values from 0.05 to 0.5
Outputs:
- new_row_emb: float32 [300, 32768], P(None, ('blk', 'grp'))
- new_row_acc: float32 [300, 32768], P(None, ('blk', 'grp'))
- new_col_emb: float32 [300, 262144], P(None, ('blk', 'grp'))
- new_col_acc: float32 [300, 262144], P(None, ('blk', 'grp'))
The draws below stay inside these ranges and needn't reach their ends.
All inputs are finite; a program needn't handle non-finite values.
Results may differ from the reference program's by a relative error of at most 0.0003.
Values sent between devices are 32-bit elements; how exact they have to be, the bound alone decides.
No kernel may reach another device: no remote copies, remote signals or barrier semaphores. Data moves between devices by JAX's collectives and lax.ppermute only.
A program may use at most 32 MiB of HBM per device.

```python
import math
import jax
import jax.numpy as jnp
from jax import lax

D = 300
ROW_DEV = 1024
VISITS = 4
ROWS = 32768
GRP_COLS = 8192
COLS = 262144
N_BLK = 32


def draw_counts(key, part):
    key = jax.random.fold_in(key, 11)
    first_key, second_key = jax.random.split(key)
    present = jax.random.randint(first_key, (VISITS, ROWS, GRP_COLS), 0, 2)
    values = jax.random.randint(second_key, (VISITS, ROWS, GRP_COLS), 1, 201)
    return (present * values).astype(jnp.float32).astype(jnp.bfloat16)


def with_ends(array, stream_key, smallest, top_value):
    place = [jax.random.randint(jax.random.fold_in(stream_key, axis), (), 0, length) for axis, length in enumerate(array.shape)]
    longest = array.shape.index(max(array.shape))
    next_to = place[:longest] + [(place[longest] + 1) % array.shape[longest]] + place[longest + 1:]
    return array.at[tuple(place)].set(smallest).at[tuple(next_to)].set(top_value)


def shard_levels(own_key, shape, cuts, smallest, top_value):
    def one(axis_at, shards_of):
        heights = jax.random.uniform(jax.random.fold_in(jax.random.fold_in(own_key, 6), axis_at), (shards_of,), jnp.float32, smallest / len(cuts), top_value / len(cuts))
        return jnp.repeat(jnp.exp(heights), shape[axis_at] // shards_of).reshape((-1,) + (1,) * (len(shape) - axis_at - 1))

    factor_of = one(*cuts[0])
    for cut in cuts[1:]:
        factor_of = factor_of * one(*cut)
    return factor_of


def normal_values(stream_key, shape, deviation, bound, shards=(), held_as=jnp.bfloat16):
    result = deviation * jax.random.normal(stream_key, shape, jnp.float32)
    if shards:
        result = result * shard_levels(stream_key, shape, shards, -0.22, 0.18)
    return jnp.clip(result, -bound, bound).astype(held_as)


def setup_inputs(seed: int = 0) -> dict:
    keys = jax.random.split(jax.random.key(seed), 8)
    return {
        "counts": draw_counts(jax.random.fold_in(keys[7], 71), 0),
        "row_sums": with_ends(jax.random.randint(keys[1], (ROWS,), 1000, 30000), jax.random.fold_in(keys[1], 1), 1000, 29999).astype(jnp.int32),
        "col_sums": with_ends(jax.random.randint(keys[2], (COLS,), 1000, 30000), jax.random.fold_in(keys[2], 1), 1000, 29999).astype(jnp.int32),
        "row_emb": normal_values(keys[3], (D, ROWS), 0.25, 1.5, ((1, 32),), jnp.float32),
        "row_acc": jnp.clip(jnp.exp(math.log(0.5) - 2.3025851 * jax.random.uniform(keys[4], (D, ROWS), jnp.float32) ** shard_levels(keys[4], (D, ROWS), ((1, 32),), -0.2, 0.2)), 0.05, 0.5),
        "col_emb": normal_values(keys[5], (D, COLS), 0.25, 1.5, ((1, 1024),), jnp.float32),
        "col_acc": jnp.clip(jnp.exp(math.log(0.5) - 2.3025851 * jax.random.uniform(keys[6], (D, COLS), jnp.float32) ** shard_levels(keys[6], (D, COLS), ((1, 1024),), -0.2, 0.2)), 0.05, 0.5),
    }


log_total = 20.0
loss_scale = 1.0 / 256.0
step_rate = 0.1

def cell_grads(row_vecs, col_vecs, row_logs, col_logs, tile_counts):
    scores = jnp.dot(row_vecs.T, col_vecs, precision=lax.Precision.HIGHEST, preferred_element_type=jnp.float32)
    counts_real = tile_counts.astype(jnp.float32)
    target = jnp.log(jnp.maximum(counts_real, 1.0)) + log_total - row_logs[:, None] - col_logs[None, :]
    weight = 0.1 + 0.25 * jnp.sqrt(counts_real)
    residue = scores - target
    return loss_scale * jnp.where(counts_real > 0.5, weight * residue, jax.nn.sigmoid(residue))

def visit_tile(pieces):
    row_vecs, row_logs, col_vecs, col_moment, col_logs, tile_counts = pieces
    cell_grad = cell_grads(row_vecs, col_vecs, row_logs, col_logs, tile_counts)
    row_part = jnp.dot(col_vecs, cell_grad.T, precision=lax.Precision.HIGHEST, preferred_element_type=jnp.float32)
    col_grad = jnp.dot(row_vecs, cell_grad, precision=lax.Precision.HIGHEST, preferred_element_type=jnp.float32)
    new_moment = col_moment + col_grad * col_grad
    new_vecs = col_vecs - step_rate * col_grad / jnp.sqrt(new_moment)
    return (row_part, new_vecs, new_moment)

def reference(counts, row_sums, col_sums, row_emb, row_acc, col_emb, col_acc):
    blocks = N_BLK
    width = D
    row_blocks = row_emb.reshape(width, blocks, ROW_DEV).transpose(1, 0, 2)
    row_logs = jnp.log(row_sums.astype(jnp.float32)).reshape(blocks, ROW_DEV)
    col_vecs = col_emb.reshape(width, blocks, GRP_COLS).transpose(1, 0, 2)
    col_moment = col_acc.reshape(width, blocks, GRP_COLS).transpose(1, 0, 2)
    col_logs = jnp.log(col_sums.astype(jnp.float32)).reshape(blocks, GRP_COLS)
    tiles = counts.reshape(VISITS, blocks, ROW_DEV, GRP_COLS)
    row_total = jnp.zeros((blocks, width, ROW_DEV), jnp.float32)
    for turn_index in range(VISITS):
        if turn_index > 0:
            col_vecs = jnp.roll(col_vecs, 1, axis=0)
            col_moment = jnp.roll(col_moment, 1, axis=0)
            col_logs = jnp.roll(col_logs, 1, axis=0)
        row_part, col_vecs, col_moment = lax.map(visit_tile, (row_blocks, row_logs, col_vecs, col_moment, col_logs, tiles[turn_index]))
        row_total = row_total + row_part
    row_grad = row_total.transpose(1, 0, 2).reshape(width, ROWS)
    new_row_acc = row_acc + row_grad * row_grad
    new_row_emb = row_emb - step_rate * row_grad / jnp.sqrt(new_row_acc)
    new_col_emb = col_vecs.transpose(1, 0, 2).reshape(width, COLS)
    new_col_acc = col_moment.transpose(1, 0, 2).reshape(width, COLS)
    return (new_row_emb, new_row_acc, new_col_emb, new_col_acc)
```

```python
import jax
import jax.numpy as jnp
from jax import lax
from jax.experimental import pallas as pl
from jax.experimental.pallas import tpu as pltpu
from jax.sharding import PartitionSpec as P

log_total = 20.0
loss_scale = 1.0 / 256.0
step_rate = 0.1

WIDTH = 300
PADW = 304
LANES = 384
ROWS = 1024
HALF = 128
TILE = 256
SHARE = 32
PACK = 40

f32 = jnp.float32
bf16 = jnp.bfloat16
VM = pl.BlockSpec(memory_space=pltpu.VMEM)
FAR = pl.BlockSpec(memory_space=pl.ANY)


def split(value):
    high = value.astype(bf16)
    return high, (value - high.astype(f32)).astype(bf16)


def dot(left, right):
    return jnp.dot(left, right, preferred_element_type=f32)


def call(name, body, out, operands, scratch=(), far=0, room=4):
    specs = [FAR] * far + [VM] * (len(operands) - far)
    spaces = [pltpu.HBM] * far + [pltpu.VMEM] * (len(operands) - far)
    placed = [pltpu.with_memory_space_constraint(each, space) for each, space in zip(operands, spaces)]
    return pl.pallas_call(
        body,
        out_shape=out,
        in_specs=specs,
        out_specs=jax.tree.map(lambda _: VM, out),
        scratch_shapes=list(scratch),
        compiler_params=pltpu.CompilerParams(vmem_limit_bytes=room * 1024 * 1024),
        cost_estimate=pl.CostEstimate(flops=1 << 20, bytes_accessed=1 << 10, transcendentals=0),
        name=name,
    )(*placed)


def near(*dims, of=f32):
    return pltpu.VMEM(dims, of)


def free(*dims, of=f32):
    return jax.ShapeDtypeStruct(dims, of)


def fetch(source, target, done):
    copy = pltpu.make_async_copy(source, target, done)
    copy.start()
    return copy


def count_tables(counts_ref, logs_ref, target_ref, weight_ref):
    for at in range(0, ROWS, TILE):
        base = logs_ref[at : at + TILE, :]
        for side in range(0, 2 * HALF, HALF):
            counts = counts_ref[at : at + TILE, side : side + HALF].astype(f32)
            target_ref[at : at + TILE, side : side + HALF] = jnp.log(jnp.maximum(counts, 1.0)) + base
            weight = loss_scale * (0.1 + 0.25 * jnp.sqrt(counts))
            weight_ref[at : at + TILE, side : side + HALF] = jnp.where(counts > 0.5, weight, 0.0)


def prep_body(
    row_hbm, counts_hbm, vecs_hbm, moment_hbm, row_sums_ref, col_sums_ref,
    hi_ref, lo_ref, turned_hi_ref, turned_lo_ref, logs_ref, target_ref, weight_ref, left_ref, right_ref,
    given_ref, row_ref, counts_ref, vecs_ref, moment_ref, done,
):
    get_counts = fetch(counts_hbm.at[0], counts_ref, done.at[0])
    get_rows = fetch(row_hbm, given_ref, done.at[1])
    get_vecs = fetch(vecs_hbm, vecs_ref, done.at[2])
    get_moment = fetch(moment_hbm, moment_ref, done.at[3])
    logs = log_total - jnp.log(row_sums_ref[...].astype(f32))
    logs_ref[...] = jnp.broadcast_to(logs, (HALF, ROWS)).T
    row_ref[WIDTH:, :] = jnp.zeros((LANES - WIDTH, ROWS), f32)
    get_counts.wait()
    count_tables(counts_ref, logs_ref, target_ref, weight_ref)
    get_rows.wait()
    row_ref[0:WIDTH, :] = given_ref[...]
    high, low = split(given_ref[...])
    hi_ref[...] = high
    lo_ref[...] = low
    for at in range(0, ROWS, TILE):
        high, low = split(row_ref[:, at : at + TILE].T)
        turned_hi_ref[at : at + TILE, :] = high
        turned_lo_ref[at : at + TILE, :] = low
    get_vecs.wait()
    get_moment.wait()
    for side, ref in enumerate((left_ref, right_ref)):
        lanes = slice(side * HALF, (side + 1) * HALF)
        ref[0:WIDTH, :] = vecs_ref[:, lanes]
        ref[WIDTH:PADW, :] = jnp.broadcast_to(jnp.log(col_sums_ref[:, lanes].astype(f32)), (PADW - WIDTH, HALF))
        ref[PADW : PADW + WIDTH, :] = moment_ref[:, lanes]
        ref[PADW + WIDTH :, :] = jnp.zeros((PADW - WIDTH, HALF), f32)


def shares_body(row_hbm, acc_hbm, vecs_ref, moment_ref, given_ref, block_ref, turned_ref, done):
    group = lax.axis_index("grp")
    lanes = pl.ds(pl.multiple_of((group >> 2) * 128, 128), 128)
    gets = [fetch(source.at[:, lanes], given_ref.at[at], done.at[at]) for at, source in enumerate((row_hbm, acc_hbm))]
    for at, ref in enumerate((vecs_ref, moment_ref)):
        gets[at].wait()
        block_ref[0:WIDTH, :] = given_ref[at]
        block_ref[WIDTH:, :] = jnp.zeros((LANES - WIDTH, 128), f32)
        turned_ref[...] = block_ref[...].T
        ref[...] = turned_ref[pl.ds(pl.multiple_of((group & 3) * SHARE, SHARE), SHARE), 0:WIDTH]


def split_columns(vecs, both_ref):
    inside = lax.broadcasted_iota(jnp.int32, (PADW, HALF), 0) < WIDTH
    high, low = split(jnp.where(inside, vecs, 0.0))
    both_ref[0:PADW, 0:HALF] = high
    both_ref[0:PADW, HALF:] = low
    both_ref[PADW:, :] = jnp.zeros((LANES - PADW, 2 * HALF), bf16)


def cells(col_logs, both_ref, turned_hi_ref, turned_lo_ref, target_ref, weight_ref, grad_ref, side):
    for at in range(0, ROWS, TILE):
        rows = slice(at, at + TILE)
        lanes = slice(side * HALF, (side + 1) * HALF)
        wide = dot(turned_hi_ref[rows, :], both_ref[...])
        scores = wide[:, :HALF] + wide[:, HALF:] + dot(turned_lo_ref[rows, :], both_ref[:, :HALF])
        residue = scores - (target_ref[rows, lanes] - col_logs)
        weight = weight_ref[rows, lanes]
        seen = weight * residue
        unseen = loss_scale / (1.0 + jnp.exp(-residue))
        high, low = split(jnp.where(weight > 0.0, seen, unseen))
        grad_ref[rows, :HALF] = high
        grad_ref[rows, HALF:] = low


def col_grads(hi_ref, lo_ref, grad_ref):
    wide = dot(hi_ref[...], grad_ref[...])
    return wide[:, :HALF] + wide[:, HALF:] + dot(lo_ref[...], grad_ref[:, :HALF])


def updated(vecs, moment, grad):
    new_moment = moment + grad * grad
    return vecs - step_rate * grad / jnp.sqrt(new_moment), new_moment


def visit_body(side, apart, state_ref, turned_hi_ref, turned_lo_ref, hi_ref, lo_ref, target_ref, weight_ref, *refs):
    grad_ref, both_ref = refs[-2:]
    if not apart:
        next_ref = refs[0]
        moment_ref = next_ref.at[PADW:]
    elif side == 0:
        next_ref, moment_ref = refs[:2]
    else:
        next_ref, pair_ref = refs[1:3]
        pair_ref[0:PADW, :] = refs[0][...]
        moment_ref = pair_ref.at[PADW:]
    split_columns(state_ref[0:PADW, :], both_ref)
    cells(state_ref[WIDTH : WIDTH + 1, :], both_ref, turned_hi_ref, turned_lo_ref, target_ref, weight_ref, grad_ref, side)
    grad = col_grads(hi_ref, lo_ref, grad_ref)
    vecs, moment = updated(state_ref[0:WIDTH, :], state_ref[PADW : PADW + WIDTH, :], grad)
    next_ref[0:WIDTH, :] = vecs
    next_ref[WIDTH:PADW, :] = state_ref[WIDTH:PADW, :]
    moment_ref[0:WIDTH, :] = moment
    moment_ref[WIDTH:, :] = jnp.zeros((PADW - WIDTH, HALF), f32)


def last_update_body(vecs_a_ref, vecs_b_ref, moments_ref, grad_a_ref, grad_b_ref, hi_ref, lo_ref, new_ref, new_moment_ref):
    for side, (vecs_ref, grad_ref) in enumerate(((vecs_a_ref, grad_a_ref), (vecs_b_ref, grad_b_ref))):
        grad = col_grads(hi_ref, lo_ref, grad_ref)
        vecs, moment = updated(vecs_ref[0:WIDTH, :], moments_ref[side * PADW : side * PADW + WIDTH, :], grad)
        new_ref[:, side * HALF : (side + 1) * HALF] = vecs
        new_moment_ref[:, side * HALF : (side + 1) * HALF] = moment


def spread(vecs_ref, high_ref, low_ref):
    main_high, main_low = split(vecs_ref[0:256, :])
    tail = vecs_ref[256:PADW, :]
    inside = lax.broadcasted_iota(jnp.int32, (PADW - 256, HALF), 0) < WIDTH - 256
    tail_high, tail_low = split(jnp.where(inside, tail, 0.0))
    gap = jnp.zeros((64 - (PADW - 256), HALF), bf16)
    places = ((high_ref, 0, main_high, tail_high), (high_ref, HALF, main_high, tail_high), (low_ref, 0, main_low, tail_low))
    for ref, at, main, rest in places:
        ref[0:256, at : at + HALF] = main
        for start in (256, 320):
            ref[start : start + PADW - 256, at : at + HALF] = rest
            ref[start + PADW - 256 : start + 64, at : at + HALF] = gap


def row_part(grad_ref, high_ref, low_ref, rows):
    by_columns = (((1,), (1,)), ((), ()))
    part = lax.dot_general(grad_ref[rows, :], high_ref[...], by_columns, preferred_element_type=f32)
    return part + lax.dot_general(grad_ref[rows, :HALF], low_ref[...], by_columns, preferred_element_type=f32)


SPREAD = [pltpu.VMEM((LANES, 2 * HALF), bf16), pltpu.VMEM((LANES, HALF), bf16)]


def beside_body(
    turn, counts_hbm, vecs_a_ref, vecs_b_ref, grad_a_ref, grad_b_ref, logs_ref, *refs
):
    before_ref = refs[0] if turn else None
    total_ref, target_ref, weight_ref, counts_ref, high_a_ref, low_a_ref, high_b_ref, low_b_ref, done = refs[1 if turn else 0 :]
    get_counts = fetch(counts_hbm.at[turn + 1], counts_ref, done)
    spread(vecs_a_ref, high_a_ref, low_a_ref)
    spread(vecs_b_ref, high_b_ref, low_b_ref)
    for at in range(0, ROWS, TILE):
        rows = slice(at, at + TILE)
        part = row_part(grad_a_ref, high_a_ref, low_a_ref, rows) + row_part(grad_b_ref, high_b_ref, low_b_ref, rows)
        total_ref[rows, :] = before_ref[rows, :] + part if turn else part
    get_counts.wait()
    count_tables(counts_ref, logs_ref, target_ref, weight_ref)


def last_half(side, vecs_ref, turned_hi_ref, turned_lo_ref, target_ref, weight_ref, before_ref, grad_ref, total_ref, both_ref, high_ref, low_ref):
    split_columns(vecs_ref[0:PADW, :], both_ref)
    cells(vecs_ref[WIDTH : WIDTH + 1, :], both_ref, turned_hi_ref, turned_lo_ref, target_ref, weight_ref, grad_ref, side)
    spread(vecs_ref, high_ref, low_ref)
    for at in range(0, ROWS, TILE):
        rows = slice(at, at + TILE)
        total_ref[rows, :] = before_ref[rows, :] + row_part(grad_ref, high_ref, low_ref, rows)


def last_body(side, vecs_ref, turned_hi_ref, turned_lo_ref, target_ref, weight_ref, before_ref, grad_ref, keep_ref, send_ref, total_ref, *scratch):
    last_half(side, vecs_ref, turned_hi_ref, turned_lo_ref, target_ref, weight_ref, before_ref, grad_ref, total_ref, *scratch)
    core = lax.axis_index("grp") & 1
    left = lax.broadcasted_iota(jnp.int32, (8, 128), 1) < 64
    for ref, half in ((keep_ref, core), (send_ref, 1 - core)):
        for slot in range(16):
            base = pl.multiple_of(slot * 2 * SHARE + half * SHARE, SHARE)
            block = total_ref[pl.ds(base, SHARE), :]
            ref[slot * PACK : slot * PACK + SHARE, :] = block[:, :256]
            for pair in range(2):
                upper = block[pair * 16 : pair * 16 + 8, 256:]
                lower = block[pair * 16 + 8 : pair * 16 + 16, 256:]
                ref[slot * PACK + SHARE : (slot + 1) * PACK, pair * 128 : (pair + 1) * 128] = jnp.where(left, upper, lower)


def halves_body(keep_ref, got_ref, leaving_ref, staying_ref):
    half = 8 * PACK
    along_x = lax.axis_index("grp") >> 4
    for ref, at in ((leaving_ref, 1 - along_x), (staying_ref, along_x)):
        rows = pl.ds(pl.multiple_of(at * half, half), half)
        ref[...] = keep_ref[rows, :] + got_ref[rows, :]


def sum_body(new_ref, new_moment_ref, left_ref, right_ref, out_ref):
    for slot in range(8):
        rows = slice(slot * PACK, (slot + 1) * PACK)
        out_ref[slot] = left_ref[rows, :] + right_ref[rows, :]


def finish_body(parts_ref, vecs_ref, moment_ref, new_ref, new_moment_ref, grad_ref):
    total = parts_ref[0]
    for at in range(1, parts_ref.shape[0]):
        total = total + parts_ref[at]
    grad_ref[:, :256] = total[0:SHARE, :]
    for group in range(4):
        rest = total[SHARE:PACK, (group // 2) * 128 : (group // 2 + 1) * 128]
        if group % 2:
            rest = pltpu.roll(rest, 64, 1)
        grad_ref[group * 8 : (group + 1) * 8, 256:] = rest
    vecs, moment = updated(vecs_ref[...], moment_ref[...], grad_ref[:, :WIDTH])
    new_ref[...] = vecs
    new_moment_ref[...] = moment


def shifted(value):
    count = lax.axis_size("blk")
    return lax.ppermute(value, "blk", [(source, (source + 1) % count) for source in range(count)])


def swapped(value, bit):
    count = lax.axis_size("grp")
    return lax.ppermute(value, "grp", [(source, source ^ bit) for source in range(count)])


def shards(counts, row_sums, col_sums, row_emb, row_acc, col_emb, col_acc):
    visits = counts.shape[0]
    cell_half = near(ROWS, 2 * HALF, of=bf16)
    table = near(ROWS, 2 * HALF)
    both = pltpu.VMEM((LANES, 2 * HALF), bf16)

    hi, lo, turned_hi, turned_lo, row_logs, target, weight, *states = call(
        "prep",
        prep_body,
        (near(WIDTH, ROWS, of=bf16),) * 2 + (near(ROWS, LANES, of=bf16),) * 2 + (near(ROWS, HALF), table, table) + (near(2 * PADW, HALF),) * 2,
        (row_emb, counts, col_emb, col_acc, row_sums.reshape(1, ROWS), col_sums.reshape(1, 2 * HALF)),
        [
            pltpu.VMEM((WIDTH, ROWS), f32),
            pltpu.VMEM((LANES, ROWS), f32),
            pltpu.VMEM((ROWS, 2 * HALF), bf16),
            pltpu.VMEM((WIDTH, 2 * HALF), f32),
            pltpu.VMEM((WIDTH, 2 * HALF), f32),
            pltpu.SemaphoreType.DMA((4,)),
        ],
        far=4,
        room=6,
    )

    total = ()
    for turn in range(visits - 1):
        nexts, grads = [], []
        apart = turn == visits - 2
        first = ()
        for side in range(2):
            outs = (near(2 * PADW, HALF),)
            if apart:
                outs = (near(PADW, HALF), near((1 + side) * PADW, HALF))
            after, *moment, grad = call(
                "visit",
                lambda *refs, side=side, apart=apart: visit_body(side, apart, *refs),
                outs + (cell_half,),
                (states[side], turned_hi, turned_lo, hi, lo, target, weight, *first),
                [both],
            )
            grads.append(grad)
            nexts.append(shifted(after))
            first = moment
        *total, target, weight = call(
            "beside",
            lambda *refs, turn=turn: beside_body(turn, *refs),
            (near(ROWS, LANES), table, table),
            (counts, states[0], states[1], grads[0], grads[1], row_logs, *total),
            [pltpu.VMEM((ROWS, 2 * HALF), bf16)] + SPREAD * 2 + [pltpu.SemaphoreType.DMA(())],
            far=1,
        )
        states = nexts

    vecs = states
    moments = shifted(moment[0])
    grad_a, part = call(
        "last_first",
        lambda *refs: last_half(0, *refs),
        (cell_half, near(ROWS, LANES)),
        (vecs[0], turned_hi, turned_lo, target, weight, *total),
        [both] + SPREAD,
    )
    grad_b, keep, send = call(
        "last_second",
        lambda *refs: last_body(1, *refs),
        (cell_half, near(16 * PACK, 256), near(16 * PACK, 256)),
        (vecs[1], turned_hi, turned_lo, target, weight, part),
        [pltpu.VMEM((ROWS, LANES), f32), both] + SPREAD,
        room=6,
    )
    new_col_emb, new_col_acc = call(
        "last_update",
        last_update_body,
        (free(WIDTH, 2 * HALF), free(WIDTH, 2 * HALF)),
        (vecs[0], vecs[1], moments, grad_a, grad_b, hi, lo),
    )

    got = swapped(send, 1)
    leaving, staying = call(
        "halves",
        halves_body,
        (near(8 * PACK, 256), near(8 * PACK, 256)),
        (keep, got),
    )
    arrived = swapped(leaving, 16)
    share = call("sum", sum_body, near(8, PACK, 256), (new_col_emb, new_col_acc, staying, arrived), far=2)
    rings = [[along_x * 16 + along_y * 2 + core for along_y in range(8)] for along_x in range(2) for core in range(2)]
    parts = lax.all_to_all(share, "grp", 0, 0, axis_index_groups=rings)

    own_vecs, own_moment = call(
        "shares",
        shares_body,
        (near(SHARE, WIDTH), near(SHARE, WIDTH)),
        (row_emb, row_acc),
        [pltpu.VMEM((2, WIDTH, 128), f32), pltpu.VMEM((LANES, 128), f32), pltpu.VMEM((128, LANES), f32), pltpu.SemaphoreType.DMA((2,))],
        far=2,
    )
    new_rows, new_row_moment = call(
        "finish",
        finish_body,
        (free(SHARE, WIDTH), free(SHARE, WIDTH)),
        (parts, own_vecs, own_moment),
        [pltpu.VMEM((SHARE, LANES), f32)],
    )
    return (new_rows.T, new_row_moment.T, new_col_emb, new_col_acc)


def solution(mesh):
    return jax.shard_map(
        shards,
        mesh=mesh,
        in_specs=(
            P(None, "blk", "grp"),
            P("blk"),
            P(("blk", "grp")),
            P(None, "blk"),
            P(None, "blk"),
            P(None, ("blk", "grp")),
            P(None, ("blk", "grp")),
        ),
        out_specs=(
            P(None, ("blk", "grp")),
            P(None, ("blk", "grp")),
            P(None, ("blk", "grp")),
            P(None, ("blk", "grp")),
        ),
        check_vma=False,
    )
```

```python
import jax
import jax.numpy as jnp
from jax import lax
from jax.experimental import pallas as pl
from jax.experimental.pallas import tpu as pltpu
from jax.sharding import PartitionSpec as P

log_total = 20.0
loss_scale = 1.0 / 256.0
step_rate = 0.1

WIDTH = 300
PADW = 304
LANES = 384
ROWS = 1024
HALF = 128
TILE = 256
SHARE = 32
PACK = 40

f32 = jnp.float32
bf16 = jnp.bfloat16
VM = pl.BlockSpec(memory_space=pltpu.VMEM)
FAR = pl.BlockSpec(memory_space=pl.ANY)


def split(value):
    high = value.astype(bf16)
    return high, (value - high.astype(f32)).astype(bf16)


def dot(left, right):
    return jnp.dot(left, right, preferred_element_type=f32)


def call(name, body, out, operands, scratch=(), far=0, room=4):
    specs = [FAR] * far + [VM] * (len(operands) - far)
    spaces = [pltpu.HBM] * far + [pltpu.VMEM] * (len(operands) - far)
    placed = [pltpu.with_memory_space_constraint(each, space) for each, space in zip(operands, spaces)]
    return pl.pallas_call(
        body,
        out_shape=out,
        in_specs=specs,
        out_specs=jax.tree.map(lambda _: VM, out),
        scratch_shapes=list(scratch),
        compiler_params=pltpu.CompilerParams(vmem_limit_bytes=room * 1024 * 1024),
        cost_estimate=pl.CostEstimate(flops=1 << 20, bytes_accessed=1 << 10, transcendentals=0),
        name=name,
    )(*placed)


def near(*dims, of=f32):
    return pltpu.VMEM(dims, of)


def free(*dims, of=f32):
    return jax.ShapeDtypeStruct(dims, of)


def fetch(source, target, done):
    copy = pltpu.make_async_copy(source, target, done)
    copy.start()
    return copy


def count_tables(counts_ref, logs_ref, target_ref, weight_ref):
    for at in range(0, ROWS, TILE):
        base = logs_ref[at : at + TILE, :]
        for side in range(0, 2 * HALF, HALF):
            counts = counts_ref[at : at + TILE, side : side + HALF].astype(f32)
            target_ref[at : at + TILE, side : side + HALF] = jnp.log(jnp.maximum(counts, 1.0)) + base
            weight = loss_scale * (0.1 + 0.25 * jnp.sqrt(counts))
            weight_ref[at : at + TILE, side : side + HALF] = jnp.where(counts > 0.5, weight, 0.0)


def prep_body(
    row_hbm, counts_hbm, vecs_hbm, moment_hbm, row_sums_hbm, col_sums_hbm,
    hi_ref, lo_ref, turned_hi_ref, turned_lo_ref, logs_ref, target_ref, weight_ref, left_ref, right_ref,
    given_ref, row_ref, counts_ref, vecs_ref, moment_ref, row_sums_ref, col_sums_ref, done,
):
    get_row_sums = fetch(row_sums_hbm, row_sums_ref, done.at[4])
    get_counts = fetch(counts_hbm.at[0], counts_ref, done.at[0])
    get_rows = fetch(row_hbm, given_ref, done.at[1])
    get_vecs = fetch(vecs_hbm, vecs_ref, done.at[2])
    get_moment = fetch(moment_hbm, moment_ref, done.at[3])
    get_col_sums = fetch(col_sums_hbm, col_sums_ref, done.at[5])
    get_row_sums.wait()
    logs = log_total - jnp.log(row_sums_ref[...].astype(f32))
    logs_ref[...] = jnp.broadcast_to(logs, (HALF, ROWS)).T
    row_ref[WIDTH:, :] = jnp.zeros((LANES - WIDTH, ROWS), f32)
    get_counts.wait()
    count_tables(counts_ref, logs_ref, target_ref, weight_ref)
    get_rows.wait()
    row_ref[0:WIDTH, :] = given_ref[...]
    high, low = split(given_ref[...])
    hi_ref[...] = high
    lo_ref[...] = low
    for at in range(0, ROWS, TILE):
        high, low = split(row_ref[:, at : at + TILE].T)
        turned_hi_ref[at : at + TILE, :] = high
        turned_lo_ref[at : at + TILE, :] = low
    get_vecs.wait()
    get_moment.wait()
    get_col_sums.wait()
    for side, ref in enumerate((left_ref, right_ref)):
        lanes = slice(side * HALF, (side + 1) * HALF)
        ref[0:WIDTH, :] = vecs_ref[:, lanes]
        ref[WIDTH:PADW, :] = jnp.broadcast_to(jnp.log(col_sums_ref[:, lanes].astype(f32)), (PADW - WIDTH, HALF))
        ref[PADW : PADW + WIDTH, :] = moment_ref[:, lanes]
        ref[PADW + WIDTH :, :] = jnp.zeros((PADW - WIDTH, HALF), f32)


def shares_body(row_hbm, acc_hbm, vecs_ref, moment_ref, given_ref, block_ref, turned_ref, done):
    group = lax.axis_index("grp")
    lanes = pl.ds(pl.multiple_of((group >> 2) * 128, 128), 128)
    gets = [fetch(source.at[:, lanes], given_ref.at[at], done.at[at]) for at, source in enumerate((row_hbm, acc_hbm))]
    for at, ref in enumerate((vecs_ref, moment_ref)):
        gets[at].wait()
        block_ref[0:WIDTH, :] = given_ref[at]
        block_ref[WIDTH:, :] = jnp.zeros((LANES - WIDTH, 128), f32)
        turned_ref[...] = block_ref[...].T
        ref[...] = turned_ref[pl.ds(pl.multiple_of((group & 3) * SHARE, SHARE), SHARE), 0:WIDTH]


def split_columns(vecs, both_ref):
    inside = lax.broadcasted_iota(jnp.int32, (PADW, HALF), 0) < WIDTH
    high, low = split(jnp.where(inside, vecs, 0.0))
    both_ref[0:PADW, 0:HALF] = high
    both_ref[0:PADW, HALF:] = low
    both_ref[PADW:, :] = jnp.zeros((LANES - PADW, 2 * HALF), bf16)


def cells(col_logs, both_ref, turned_hi_ref, turned_lo_ref, target_ref, weight_ref, grad_ref, side):
    for at in range(0, ROWS, TILE):
        rows = slice(at, at + TILE)
        lanes = slice(side * HALF, (side + 1) * HALF)
        wide = dot(turned_hi_ref[rows, :], both_ref[...])
        scores = wide[:, :HALF] + wide[:, HALF:] + dot(turned_lo_ref[rows, :], both_ref[:, :HALF])
        residue = scores - (target_ref[rows, lanes] - col_logs)
        weight = weight_ref[rows, lanes]
        seen = weight * residue
        unseen = loss_scale / (1.0 + jnp.exp(-residue))
        high, low = split(jnp.where(weight > 0.0, seen, unseen))
        grad_ref[rows, :HALF] = high
        grad_ref[rows, HALF:] = low


def col_grads(hi_ref, lo_ref, grad_ref):
    wide = dot(hi_ref[...], grad_ref[...])
    return wide[:, :HALF] + wide[:, HALF:] + dot(lo_ref[...], grad_ref[:, :HALF])


def updated(vecs, moment, grad):
    new_moment = moment + grad * grad
    return vecs - step_rate * grad / jnp.sqrt(new_moment), new_moment


def visit_body(side, state_ref, turned_hi_ref, turned_lo_ref, hi_ref, lo_ref, target_ref, weight_ref, next_ref, grad_ref, both_ref):
    split_columns(state_ref[0:PADW, :], both_ref)
    cells(state_ref[WIDTH : WIDTH + 1, :], both_ref, turned_hi_ref, turned_lo_ref, target_ref, weight_ref, grad_ref, side)
    grad = col_grads(hi_ref, lo_ref, grad_ref)
    vecs, moment = updated(state_ref[0:WIDTH, :], state_ref[PADW : PADW + WIDTH, :], grad)
    next_ref[0:WIDTH, :] = vecs
    next_ref[WIDTH:PADW, :] = state_ref[WIDTH:PADW, :]
    next_ref[PADW : PADW + WIDTH, :] = moment
    next_ref[PADW + WIDTH :, :] = jnp.zeros((PADW - WIDTH, HALF), f32)


def last_update_body(state_a_ref, state_b_ref, grad_a_ref, grad_b_ref, hi_ref, lo_ref, new_ref, new_moment_ref):
    for side, (state_ref, grad_ref) in enumerate(((state_a_ref, grad_a_ref), (state_b_ref, grad_b_ref))):
        grad = col_grads(hi_ref, lo_ref, grad_ref)
        vecs, moment = updated(state_ref[0:WIDTH, :], state_ref[PADW : PADW + WIDTH, :], grad)
        new_ref[:, side * HALF : (side + 1) * HALF] = vecs
        new_moment_ref[:, side * HALF : (side + 1) * HALF] = moment


def spread(vecs_ref, high_ref, low_ref):
    main_high, main_low = split(vecs_ref[0:256, :])
    tail = vecs_ref[256:PADW, :]
    inside = lax.broadcasted_iota(jnp.int32, (PADW - 256, HALF), 0) < WIDTH - 256
    tail_high, tail_low = split(jnp.where(inside, tail, 0.0))
    gap = jnp.zeros((64 - (PADW - 256), HALF), bf16)
    places = ((high_ref, 0, main_high, tail_high), (high_ref, HALF, main_high, tail_high), (low_ref, 0, main_low, tail_low))
    for ref, at, main, rest in places:
        ref[0:256, at : at + HALF] = main
        for start in (256, 320):
            ref[start : start + PADW - 256, at : at + HALF] = rest
            ref[start + PADW - 256 : start + 64, at : at + HALF] = gap


def row_part(grad_ref, high_ref, low_ref, rows):
    by_columns = (((1,), (1,)), ((), ()))
    part = lax.dot_general(grad_ref[rows, :], high_ref[...], by_columns, preferred_element_type=f32)
    return part + lax.dot_general(grad_ref[rows, :HALF], low_ref[...], by_columns, preferred_element_type=f32)


SPREAD = [pltpu.VMEM((LANES, 2 * HALF), bf16), pltpu.VMEM((LANES, HALF), bf16)]


def beside_body(
    turn, counts_hbm, vecs_a_ref, vecs_b_ref, grad_a_ref, grad_b_ref, logs_ref, *refs
):
    before_ref = refs[0] if turn else None
    total_ref, target_ref, weight_ref, counts_ref, high_a_ref, low_a_ref, high_b_ref, low_b_ref, done = refs[1 if turn else 0 :]
    get_counts = fetch(counts_hbm.at[turn + 1], counts_ref, done)
    spread(vecs_a_ref, high_a_ref, low_a_ref)
    spread(vecs_b_ref, high_b_ref, low_b_ref)
    for at in range(0, ROWS, TILE):
        rows = slice(at, at + TILE)
        part = row_part(grad_a_ref, high_a_ref, low_a_ref, rows) + row_part(grad_b_ref, high_b_ref, low_b_ref, rows)
        total_ref[rows, :] = before_ref[rows, :] + part if turn else part
    get_counts.wait()
    count_tables(counts_ref, logs_ref, target_ref, weight_ref)


def last_half(side, vecs_ref, turned_hi_ref, turned_lo_ref, target_ref, weight_ref, before_ref, grad_ref, total_ref, both_ref, high_ref, low_ref):
    split_columns(vecs_ref[0:PADW, :], both_ref)
    cells(vecs_ref[WIDTH : WIDTH + 1, :], both_ref, turned_hi_ref, turned_lo_ref, target_ref, weight_ref, grad_ref, side)
    spread(vecs_ref, high_ref, low_ref)
    for at in range(0, ROWS, TILE):
        rows = slice(at, at + TILE)
        total_ref[rows, :] = before_ref[rows, :] + row_part(grad_ref, high_ref, low_ref, rows)


def last_body(side, vecs_ref, turned_hi_ref, turned_lo_ref, target_ref, weight_ref, before_ref, grad_ref, keep_ref, send_ref, total_ref, *scratch):
    last_half(side, vecs_ref, turned_hi_ref, turned_lo_ref, target_ref, weight_ref, before_ref, grad_ref, total_ref, *scratch)
    core = lax.axis_index("grp") & 1
    left = lax.broadcasted_iota(jnp.int32, (8, 128), 1) < 64
    for ref, half in ((keep_ref, core), (send_ref, 1 - core)):
        for slot in range(16):
            place = (slot & 8) + 2 * (slot & 3) + ((slot >> 2) & 1)
            base = pl.multiple_of(place * 2 * SHARE + half * SHARE, SHARE)
            block = total_ref[pl.ds(base, SHARE), :]
            ref[slot * PACK : slot * PACK + SHARE, :] = block[:, :256]
            for pair in range(2):
                upper = block[pair * 16 : pair * 16 + 8, 256:]
                lower = block[pair * 16 + 8 : pair * 16 + 16, 256:]
                ref[slot * PACK + SHARE : (slot + 1) * PACK, pair * 128 : (pair + 1) * 128] = jnp.where(left, upper, lower)


def quarters_body(keep_ref, got_ref, own_ref, *others):
    group = lax.axis_index("grp")
    quarter = 2 * (group >> 4) + ((group >> 1) & 1)
    size = 4 * PACK
    for at, ref in enumerate((own_ref, *others)):
        rows = pl.ds(pl.multiple_of((quarter ^ at) * size, size), size)
        ref[...] = keep_ref[rows, :] + got_ref[rows, :]


def pieces_body(new_ref, new_moment_ref, vecs_ref, acc_ref, own_ref, first_ref, second_ref, third_ref, *outs):
    high = (lax.axis_index("grp") >> 2) & 3
    for at, ref in enumerate(outs):
        rows = pl.ds(pl.multiple_of((high ^ at) * PACK, PACK), PACK)
        ref[...] = (own_ref[rows, :] + first_ref[rows, :]) + (second_ref[rows, :] + third_ref[rows, :])


def finish_body(own_ref, first_ref, second_ref, third_ref, vecs_ref, moment_ref, new_ref, new_moment_ref, grad_ref):
    total = (own_ref[...] + first_ref[...]) + (second_ref[...] + third_ref[...])
    grad_ref[:, :256] = total[0:SHARE, :]
    for group in range(4):
        rest = total[SHARE:PACK, (group // 2) * 128 : (group // 2 + 1) * 128]
        if group % 2:
            rest = pltpu.roll(rest, 64, 1)
        grad_ref[group * 8 : (group + 1) * 8, 256:] = rest
    vecs, moment = updated(vecs_ref[...], moment_ref[...], grad_ref[:, :WIDTH])
    new_ref[...] = vecs
    new_moment_ref[...] = moment


def shifted(value):
    count = lax.axis_size("blk")
    return lax.ppermute(value, "blk", [(source, (source + 1) % count) for source in range(count)])


def swapped(value, bit):
    count = lax.axis_size("grp")
    return lax.ppermute(value, "grp", [(source, source ^ bit) for source in range(count)])


def shards(counts, row_sums, col_sums, row_emb, row_acc, col_emb, col_acc):
    visits = counts.shape[0]
    cell_half = near(ROWS, 2 * HALF, of=bf16)
    table = near(ROWS, 2 * HALF)
    both = pltpu.VMEM((LANES, 2 * HALF), bf16)

    hi, lo, turned_hi, turned_lo, row_logs, target, weight, *states = call(
        "prep",
        prep_body,
        (near(WIDTH, ROWS, of=bf16),) * 2 + (near(ROWS, LANES, of=bf16),) * 2 + (near(ROWS, HALF), table, table) + (near(2 * PADW, HALF),) * 2,
        (row_emb, counts, col_emb, col_acc, row_sums.reshape(1, ROWS), col_sums.reshape(1, 2 * HALF)),
        [
            pltpu.VMEM((WIDTH, ROWS), f32),
            pltpu.VMEM((LANES, ROWS), f32),
            pltpu.VMEM((ROWS, 2 * HALF), bf16),
            pltpu.VMEM((WIDTH, 2 * HALF), f32),
            pltpu.VMEM((WIDTH, 2 * HALF), f32),
            pltpu.VMEM((1, ROWS), jnp.int32),
            pltpu.VMEM((1, 2 * HALF), jnp.int32),
            pltpu.SemaphoreType.DMA((6,)),
        ],
        far=6,
        room=6,
    )

    total = ()
    for turn in range(visits - 1):
        nexts, grads = [], []
        for side in range(2):
            after, grad = call(
                "visit",
                lambda *refs, side=side: visit_body(side, *refs),
                (near(2 * PADW, HALF), cell_half),
                (states[side], turned_hi, turned_lo, hi, lo, target, weight),
                [both],
            )
            grads.append(grad)
            nexts.append(shifted(after))
        *total, target, weight = call(
            "beside",
            lambda *refs, turn=turn: beside_body(turn, *refs),
            (near(ROWS, LANES), table, table),
            (counts, states[0], states[1], grads[0], grads[1], row_logs, *total),
            [pltpu.VMEM((ROWS, 2 * HALF), bf16)] + SPREAD * 2 + [pltpu.SemaphoreType.DMA(())],
            far=1,
        )
        states = nexts

    grad_a, part = call(
        "last_first",
        lambda *refs: last_half(0, *refs),
        (cell_half, near(ROWS, LANES)),
        (states[0], turned_hi, turned_lo, target, weight, *total),
        [both] + SPREAD,
    )
    grad_b, keep, send = call(
        "last_second",
        lambda *refs: last_body(1, *refs),
        (cell_half, near(16 * PACK, 256), near(16 * PACK, 256)),
        (states[1], turned_hi, turned_lo, target, weight, part),
        [pltpu.VMEM((ROWS, LANES), f32), both] + SPREAD,
        room=6,
    )
    new_col_emb, new_col_acc = call(
        "last_update",
        last_update_body,
        (free(WIDTH, 2 * HALF), free(WIDTH, 2 * HALF)),
        (states[0], states[1], grad_a, grad_b, hi, lo),
    )

    own_vecs, own_moment = call(
        "shares",
        shares_body,
        (near(SHARE, WIDTH), near(SHARE, WIDTH)),
        (row_emb, row_acc),
        [pltpu.VMEM((2, WIDTH, 128), f32), pltpu.VMEM((LANES, 128), f32), pltpu.VMEM((128, LANES), f32), pltpu.SemaphoreType.DMA((2,))],
        far=2,
    )
    got = swapped(send, 1)
    own, *others = call("quarters", quarters_body, (near(4 * PACK, 256),) * 4, (keep, got))
    arrived = [swapped(each, bits) for each, bits in zip(others[::-1], (18, 16, 2))]
    before = (new_col_emb, new_col_acc, own_vecs, own_moment)
    own, *others = call("pieces", pieces_body, (near(PACK, 256),) * 4, (*before, own, *arrived), far=2)
    parts = [own] + [swapped(each, bits) for each, bits in zip(others, (4, 8, 12))]

    new_rows, new_row_moment = call(
        "finish",
        finish_body,
        (free(SHARE, WIDTH), free(SHARE, WIDTH)),
        (*parts, own_vecs, own_moment),
        [pltpu.VMEM((SHARE, LANES), f32)],
    )
    return (new_rows.T, new_row_moment.T, new_col_emb, new_col_acc)


def solution(mesh):
    return jax.shard_map(
        shards,
        mesh=mesh,
        in_specs=(
            P(None, "blk", "grp"),
            P("blk"),
            P(("blk", "grp")),
            P(None, "blk"),
            P(None, "blk"),
            P(None, ("blk", "grp")),
            P(None, ("blk", "grp")),
        ),
        out_specs=(
            P(None, ("blk", "grp")),
            P(None, ("blk", "grp")),
            P(None, ("blk", "grp")),
            P(None, ("blk", "grp")),
        ),
        check_vma=False,
    )
```

```python
import jax
import jax.numpy as jnp
from jax import lax
from jax.experimental import pallas as pl
from jax.experimental.pallas import tpu as pltpu
from jax.sharding import PartitionSpec as P

log_total = 20.0
loss_scale = 1.0 / 256.0
step_rate = 0.1

WIDTH = 300
PADW = 304
LANES = 384
ROWS = 1024
HALF = 128
TILE = 256
SHARE = 32
PACK = 40

f32 = jnp.float32
bf16 = jnp.bfloat16
VM = pl.BlockSpec(memory_space=pltpu.VMEM)
FAR = pl.BlockSpec(memory_space=pl.ANY)


def split(value):
    high = value.astype(bf16)
    return high, (value - high.astype(f32)).astype(bf16)


def dot(left, right):
    return jnp.dot(left, right, preferred_element_type=f32)


def call(name, body, out, operands, scratch=(), far=0, room=4, flops=1 << 32):
    specs = [FAR] * far + [VM] * (len(operands) - far)
    spaces = [pltpu.HBM] * far + [pltpu.VMEM] * (len(operands) - far)
    placed = [pltpu.with_memory_space_constraint(each, space) for each, space in zip(operands, spaces)]
    return pl.pallas_call(
        body,
        out_shape=out,
        in_specs=specs,
        out_specs=jax.tree.map(lambda _: VM, out),
        scratch_shapes=list(scratch),
        compiler_params=pltpu.CompilerParams(vmem_limit_bytes=room * 1024 * 1024),
        cost_estimate=pl.CostEstimate(flops=flops, bytes_accessed=1 << 10, transcendentals=0),
        name=name,
    )(*placed)


def near(*dims, of=f32):
    return pltpu.VMEM(dims, of)


def free(*dims, of=f32):
    return jax.ShapeDtypeStruct(dims, of)


def fetch(source, target, done):
    copy = pltpu.make_async_copy(source, target, done)
    copy.start()
    return copy


def count_tables(counts_ref, logs_ref, target_ref, weight_ref):
    for at in range(0, ROWS, TILE):
        base = logs_ref[at : at + TILE, :]
        for side in range(0, 2 * HALF, HALF):
            counts = counts_ref[at : at + TILE, side : side + HALF].astype(f32)
            target_ref[at : at + TILE, side : side + HALF] = jnp.log(jnp.maximum(counts, 1.0)) + base
            weight = loss_scale * (0.1 + 0.25 * jnp.sqrt(counts))
            weight_ref[at : at + TILE, side : side + HALF] = jnp.where(counts > 0.5, weight, 0.0)


def prep_body(
    row_hbm, counts_hbm, vecs_hbm, moment_hbm, row_sums_hbm, col_sums_hbm,
    hi_ref, lo_ref, turned_hi_ref, turned_lo_ref, logs_ref, target_ref, weight_ref, left_ref, right_ref,
    given_ref, row_ref, counts_ref, vecs_ref, moment_ref, row_sums_ref, col_sums_ref, done,
):
    get_row_sums = fetch(row_sums_hbm, row_sums_ref, done.at[4])
    get_counts = fetch(counts_hbm.at[0], counts_ref, done.at[0])
    get_rows = fetch(row_hbm, given_ref, done.at[1])
    get_vecs = fetch(vecs_hbm, vecs_ref, done.at[2])
    get_moment = fetch(moment_hbm, moment_ref, done.at[3])
    get_col_sums = fetch(col_sums_hbm, col_sums_ref, done.at[5])
    get_row_sums.wait()
    logs = log_total - jnp.log(row_sums_ref[...].astype(f32))
    logs_ref[...] = jnp.broadcast_to(logs, (HALF, ROWS)).T
    row_ref[WIDTH:, :] = jnp.zeros((LANES - WIDTH, ROWS), f32)
    get_counts.wait()
    count_tables(counts_ref, logs_ref, target_ref, weight_ref)
    get_rows.wait()
    row_ref[0:WIDTH, :] = given_ref[...]
    high, low = split(given_ref[...])
    hi_ref[...] = high
    lo_ref[...] = low
    for at in range(0, ROWS, TILE):
        high, low = split(row_ref[:, at : at + TILE].T)
        turned_hi_ref[at : at + TILE, :] = high
        turned_lo_ref[at : at + TILE, :] = low
    get_vecs.wait()
    get_moment.wait()
    get_col_sums.wait()
    for side, ref in enumerate((left_ref, right_ref)):
        lanes = slice(side * HALF, (side + 1) * HALF)
        ref[0:WIDTH, :] = vecs_ref[:, lanes]
        ref[WIDTH:PADW, :] = jnp.broadcast_to(jnp.log(col_sums_ref[:, lanes].astype(f32)), (PADW - WIDTH, HALF))
        ref[PADW : PADW + WIDTH, :] = moment_ref[:, lanes]
        ref[PADW + WIDTH :, :] = jnp.zeros((PADW - WIDTH, HALF), f32)


def shares_body(row_hbm, acc_hbm, vecs_ref, moment_ref, given_ref, block_ref, turned_ref, done):
    group = lax.axis_index("grp")
    lanes = pl.ds(pl.multiple_of((group >> 2) * 128, 128), 128)
    gets = [fetch(source.at[:, lanes], given_ref.at[at], done.at[at]) for at, source in enumerate((row_hbm, acc_hbm))]
    for at, ref in enumerate((vecs_ref, moment_ref)):
        gets[at].wait()
        block_ref[0:WIDTH, :] = given_ref[at]
        block_ref[WIDTH:, :] = jnp.zeros((LANES - WIDTH, 128), f32)
        turned_ref[...] = block_ref[...].T
        ref[...] = turned_ref[pl.ds(pl.multiple_of((group & 3) * SHARE, SHARE), SHARE), 0:WIDTH]


def split_columns(vecs, both_ref):
    inside = lax.broadcasted_iota(jnp.int32, (PADW, HALF), 0) < WIDTH
    high, low = split(jnp.where(inside, vecs, 0.0))
    both_ref[0:PADW, 0:HALF] = high
    both_ref[0:PADW, HALF:] = low
    both_ref[PADW:, :] = jnp.zeros((LANES - PADW, 2 * HALF), bf16)


def cells(col_logs, both_ref, turned_hi_ref, turned_lo_ref, target_ref, weight_ref, grad_ref, side):
    for at in range(0, ROWS, TILE):
        rows = slice(at, at + TILE)
        lanes = slice(side * HALF, (side + 1) * HALF)
        wide = dot(turned_hi_ref[rows, :], both_ref[...])
        scores = wide[:, :HALF] + wide[:, HALF:] + dot(turned_lo_ref[rows, :], both_ref[:, :HALF])
        residue = scores - (target_ref[rows, lanes] - col_logs)
        weight = weight_ref[rows, lanes]
        seen = weight * residue
        unseen = loss_scale / (1.0 + jnp.exp(-residue))
        high, low = split(jnp.where(weight > 0.0, seen, unseen))
        grad_ref[rows, :HALF] = high
        grad_ref[rows, HALF:] = low


def col_grads(hi_ref, lo_ref, grad_ref):
    wide = dot(hi_ref[...], grad_ref[...])
    return wide[:, :HALF] + wide[:, HALF:] + dot(lo_ref[...], grad_ref[:, :HALF])


def updated(vecs, moment, grad):
    new_moment = moment + grad * grad
    return vecs - step_rate * grad / jnp.sqrt(new_moment), new_moment


def first_visit_body(side, state_ref, turned_hi_ref, turned_lo_ref, hi_ref, lo_ref, target_ref, weight_ref, vecs_ref, moment_ref, grad_ref, both_ref):
    split_columns(state_ref[0:PADW, :], both_ref)
    cells(state_ref[WIDTH : WIDTH + 1, :], both_ref, turned_hi_ref, turned_lo_ref, target_ref, weight_ref, grad_ref, side)
    grad = col_grads(hi_ref, lo_ref, grad_ref)
    vecs, moment = updated(state_ref[0:WIDTH, :], state_ref[PADW : PADW + WIDTH, :], grad)
    vecs_ref[0:WIDTH, :] = vecs
    vecs_ref[WIDTH:, :] = state_ref[WIDTH:PADW, :]
    moment_ref[0:WIDTH, :] = moment
    moment_ref[WIDTH:, :] = jnp.zeros((PADW - WIDTH, HALF), f32)


def second_visit_body(side, vecs_ref, turned_hi_ref, turned_lo_ref, hi_ref, lo_ref, target_ref, weight_ref, out_ref, grad_ref, both_ref):
    split_columns(vecs_ref[...], both_ref)
    cells(vecs_ref[WIDTH : WIDTH + 1, :], both_ref, turned_hi_ref, turned_lo_ref, target_ref, weight_ref, grad_ref, side)
    out_ref[0:WIDTH, :] = col_grads(hi_ref, lo_ref, grad_ref)
    out_ref[WIDTH:, :] = jnp.zeros((PADW - WIDTH, HALF), f32)


def third_visit_body(side, whole_ref, sent_ref, turned_hi_ref, turned_lo_ref, hi_ref, lo_ref, target_ref, weight_ref, *refs):
    now_ref, vecs_ref, moment_ref, grad_ref, both_ref = refs
    at = side * 2 * PADW
    vecs, moment = updated(whole_ref[at : at + WIDTH, :], whole_ref[at + PADW : at + PADW + WIDTH, :], sent_ref[0:WIDTH, :])
    now_ref[0:WIDTH, :] = vecs
    now_ref[WIDTH:, :] = whole_ref[at + WIDTH : at + PADW, :]
    split_columns(now_ref[...], both_ref)
    cells(now_ref[WIDTH : WIDTH + 1, :], both_ref, turned_hi_ref, turned_lo_ref, target_ref, weight_ref, grad_ref, side)
    vecs, moment = updated(now_ref[0:WIDTH, :], moment, col_grads(hi_ref, lo_ref, grad_ref))
    vecs_ref[0:WIDTH, :] = vecs
    vecs_ref[WIDTH:, :] = now_ref[WIDTH:, :]
    moment_ref[0:WIDTH, :] = moment
    moment_ref[WIDTH:, :] = jnp.zeros((PADW - WIDTH, HALF), f32)


def last_update_body(vecs_a_ref, vecs_b_ref, moments_ref, grad_a_ref, grad_b_ref, hi_ref, lo_ref, new_ref, new_moment_ref):
    for side, (vecs_ref, grad_ref) in enumerate(((vecs_a_ref, grad_a_ref), (vecs_b_ref, grad_b_ref))):
        grad = col_grads(hi_ref, lo_ref, grad_ref)
        vecs, moment = updated(vecs_ref[0:WIDTH, :], moments_ref[side * PADW : side * PADW + WIDTH, :], grad)
        new_ref[:, side * HALF : (side + 1) * HALF] = vecs
        new_moment_ref[:, side * HALF : (side + 1) * HALF] = moment


def spread(vecs_ref, high_ref, low_ref):
    main_high, main_low = split(vecs_ref[0:256, :])
    tail = vecs_ref[256:PADW, :]
    inside = lax.broadcasted_iota(jnp.int32, (PADW - 256, HALF), 0) < WIDTH - 256
    tail_high, tail_low = split(jnp.where(inside, tail, 0.0))
    gap = jnp.zeros((64 - (PADW - 256), HALF), bf16)
    places = ((high_ref, 0, main_high, tail_high), (high_ref, HALF, main_high, tail_high), (low_ref, 0, main_low, tail_low))
    for ref, at, main, rest in places:
        ref[0:256, at : at + HALF] = main
        for start in (256, 320):
            ref[start : start + PADW - 256, at : at + HALF] = rest
            ref[start + PADW - 256 : start + 64, at : at + HALF] = gap


def row_part(grad_ref, high_ref, low_ref, rows):
    by_columns = (((1,), (1,)), ((), ()))
    part = lax.dot_general(grad_ref[rows, :], high_ref[...], by_columns, preferred_element_type=f32)
    return part + lax.dot_general(grad_ref[rows, :HALF], low_ref[...], by_columns, preferred_element_type=f32)


SPREAD = [pltpu.VMEM((LANES, 2 * HALF), bf16), pltpu.VMEM((LANES, HALF), bf16)]


def beside_body(turn, packs, counts_hbm, vecs_a_ref, vecs_b_ref, grad_a_ref, grad_b_ref, logs_ref, *refs):
    before_ref = refs[packs] if turn else None
    packed_ref = refs[-10] if packs else None
    total_ref, target_ref, weight_ref, counts_ref, high_a_ref, low_a_ref, high_b_ref, low_b_ref, done = refs[-9:]
    get_counts = fetch(counts_hbm.at[turn + 1], counts_ref, done)
    for at in range(packs):
        packed_ref[at * PADW : (at + 1) * PADW, :] = refs[at][...]
    spread(vecs_a_ref, high_a_ref, low_a_ref)
    spread(vecs_b_ref, high_b_ref, low_b_ref)
    for at in range(0, ROWS, TILE):
        rows = slice(at, at + TILE)
        part = row_part(grad_a_ref, high_a_ref, low_a_ref, rows) + row_part(grad_b_ref, high_b_ref, low_b_ref, rows)
        total_ref[rows, :] = before_ref[rows, :] + part if turn else part
    get_counts.wait()
    count_tables(counts_ref, logs_ref, target_ref, weight_ref)


def last_half(side, vecs_ref, turned_hi_ref, turned_lo_ref, target_ref, weight_ref, before_ref, grad_ref, total_ref, both_ref, high_ref, low_ref):
    split_columns(vecs_ref[0:PADW, :], both_ref)
    cells(vecs_ref[WIDTH : WIDTH + 1, :], both_ref, turned_hi_ref, turned_lo_ref, target_ref, weight_ref, grad_ref, side)
    spread(vecs_ref, high_ref, low_ref)
    for at in range(0, ROWS, TILE):
        rows = slice(at, at + TILE)
        total_ref[rows, :] = before_ref[rows, :] + row_part(grad_ref, high_ref, low_ref, rows)


def last_body(side, vecs_ref, turned_hi_ref, turned_lo_ref, target_ref, weight_ref, before_ref, grad_ref, keep_ref, send_ref, total_ref, *scratch):
    last_half(side, vecs_ref, turned_hi_ref, turned_lo_ref, target_ref, weight_ref, before_ref, grad_ref, total_ref, *scratch)
    core = lax.axis_index("grp") & 1
    left = lax.broadcasted_iota(jnp.int32, (8, 128), 1) < 64
    for ref, half in ((keep_ref, core), (send_ref, 1 - core)):
        for slot in range(16):
            base = pl.multiple_of(slot * 2 * SHARE + half * SHARE, SHARE)
            block = total_ref[pl.ds(base, SHARE), :]
            ref[slot * PACK : slot * PACK + SHARE, :] = block[:, :256]
            for pair in range(2):
                upper = block[pair * 16 : pair * 16 + 8, 256:]
                lower = block[pair * 16 + 8 : pair * 16 + 16, 256:]
                ref[slot * PACK + SHARE : (slot + 1) * PACK, pair * 128 : (pair + 1) * 128] = jnp.where(left, upper, lower)


def sum_body(new_ref, new_moment_ref, keep_ref, got_ref, out_ref):
    for slot in range(16):
        rows = slice(slot * PACK, (slot + 1) * PACK)
        out_ref[slot] = keep_ref[rows, :] + got_ref[rows, :]


def finish_body(parts_ref, vecs_ref, moment_ref, new_ref, new_moment_ref, grad_ref):
    total = parts_ref[0]
    for at in range(1, parts_ref.shape[0]):
        total = total + parts_ref[at]
    grad_ref[:, :256] = total[0:SHARE, :]
    for group in range(4):
        rest = total[SHARE:PACK, (group // 2) * 128 : (group // 2 + 1) * 128]
        if group % 2:
            rest = pltpu.roll(rest, 64, 1)
        grad_ref[group * 8 : (group + 1) * 8, 256:] = rest
    vecs, moment = updated(vecs_ref[...], moment_ref[...], grad_ref[:, :WIDTH])
    new_ref[...] = vecs
    new_moment_ref[...] = moment


def shifted(value, steps=1):
    count = lax.axis_size("blk")
    return lax.ppermute(value, "blk", [(source, (source + steps) % count) for source in range(count)])


def swapped(value, bit):
    count = lax.axis_size("grp")
    return lax.ppermute(value, "grp", [(source, source ^ bit) for source in range(count)])


def shards(counts, row_sums, col_sums, row_emb, row_acc, col_emb, col_acc):
    cell_half = near(ROWS, 2 * HALF, of=bf16)
    table = near(ROWS, 2 * HALF)
    both = pltpu.VMEM((LANES, 2 * HALF), bf16)

    hi, lo, turned_hi, turned_lo, row_logs, target, weight, *states = call(
        "prep",
        prep_body,
        (near(WIDTH, ROWS, of=bf16),) * 2 + (near(ROWS, LANES, of=bf16),) * 2 + (near(ROWS, HALF), table, table) + (near(2 * PADW, HALF),) * 2,
        (row_emb, counts, col_emb, col_acc, row_sums.reshape(1, ROWS), col_sums.reshape(1, 2 * HALF)),
        [
            pltpu.VMEM((WIDTH, ROWS), f32),
            pltpu.VMEM((LANES, ROWS), f32),
            pltpu.VMEM((ROWS, 2 * HALF), bf16),
            pltpu.VMEM((WIDTH, 2 * HALF), f32),
            pltpu.VMEM((WIDTH, 2 * HALF), f32),
            pltpu.VMEM((1, ROWS), jnp.int32),
            pltpu.VMEM((1, 2 * HALF), jnp.int32),
            pltpu.SemaphoreType.DMA((6,)),
        ],
        far=6,
        room=6,
    )

    rows = (turned_hi, turned_lo, hi, lo)

    def beside(turn, vecs, grads, packs, *more):
        packed = (near(len(packs) * PADW, HALF),) if packs else ()
        return call(
            "beside",
            lambda *refs: beside_body(turn, len(packs), *refs),
            (*packed, near(ROWS, LANES), table, table),
            (counts, *vecs, *grads, row_logs, *packs, *more),
            [pltpu.VMEM((ROWS, 2 * HALF), bf16)] + SPREAD * 2 + [pltpu.SemaphoreType.DMA(())],
            far=1,
        )

    near_vecs = near(PADW, HALF)
    vecs, moments, grads = [None] * 2, [None] * 2, [None] * 2
    for side in range(2):
        vecs[side], moments[side], grads[side] = call(
            "first_visit",
            lambda *refs, side=side: first_visit_body(side, *refs),
            (near_vecs, near_vecs, cell_half),
            (states[side], *rows, target, weight),
            [both],
        )
    whole, total, target, weight = beside(0, states, grads, (vecs[0], moments[0], vecs[1], moments[1]))
    whole = shifted(whole, 2)
    vecs = [shifted(each) for each in vecs]

    sent, grads = [None] * 2, [None] * 2
    for side in range(2):
        sent[side], grads[side] = call(
            "second_visit",
            lambda *refs, side=side: second_visit_body(side, *refs),
            (near_vecs, cell_half),
            (vecs[side], *rows, target, weight),
            [both],
        )
        sent[side] = shifted(sent[side])
    total, target, weight = beside(1, vecs, grads, (), total)

    now, vecs, grads = [None] * 2, [None] * 2, [None] * 2
    for side in range(2):
        now[side], vecs[side], moments[side], grads[side] = call(
            "third_visit",
            lambda *refs, side=side: third_visit_body(side, *refs),
            (near_vecs, near_vecs, near_vecs, cell_half),
            (whole, sent[side], *rows, target, weight),
            [both],
        )
        vecs[side] = shifted(vecs[side])
    moments, total, target, weight = beside(2, now, grads, moments, total)
    moments = shifted(moments)

    grad_a, part = call(
        "last_first",
        lambda *refs: last_half(0, *refs),
        (cell_half, near(ROWS, LANES)),
        (vecs[0], turned_hi, turned_lo, target, weight, total),
        [both] + SPREAD,
    )
    grad_b, keep, send = call(
        "last_second",
        lambda *refs: last_body(1, *refs),
        (cell_half, near(16 * PACK, 256), near(16 * PACK, 256)),
        (vecs[1], turned_hi, turned_lo, target, weight, part),
        [pltpu.VMEM((ROWS, LANES), f32), both] + SPREAD,
        room=6,
    )
    new_col_emb, new_col_acc = call(
        "last_update",
        last_update_body,
        (free(WIDTH, 2 * HALF), free(WIDTH, 2 * HALF)),
        (vecs[0], vecs[1], moments, grad_a, grad_b, hi, lo),
        flops=1 << 33,
    )

    own_vecs, own_moment = call(
        "shares",
        shares_body,
        (near(SHARE, WIDTH), near(SHARE, WIDTH)),
        (row_emb, row_acc),
        [pltpu.VMEM((2, WIDTH, 128), f32), pltpu.VMEM((LANES, 128), f32), pltpu.VMEM((128, LANES), f32), pltpu.SemaphoreType.DMA((2,))],
        far=2,
    )
    got = swapped(send, 1)
    share = call("sum", sum_body, near(16, PACK, 256), (new_col_emb, new_col_acc, keep, got), far=2)
    chips = [[2 * chip + core for chip in range(16)] for core in range(2)]
    parts = lax.all_to_all(share, "grp", 0, 0, axis_index_groups=chips)

    new_rows, new_row_moment = call(
        "finish",
        finish_body,
        (free(SHARE, WIDTH), free(SHARE, WIDTH)),
        (parts, own_vecs, own_moment),
        [pltpu.VMEM((SHARE, LANES), f32)],
    )
    return (new_rows.T, new_row_moment.T, new_col_emb, new_col_acc)


def solution(mesh):
    return jax.shard_map(
        shards,
        mesh=mesh,
        in_specs=(
            P(None, "blk", "grp"),
            P("blk"),
            P(("blk", "grp")),
            P(None, "blk"),
            P(None, "blk"),
            P(None, ("blk", "grp")),
            P(None, ("blk", "grp")),
        ),
        out_specs=(
            P(None, ("blk", "grp")),
            P(None, ("blk", "grp")),
            P(None, ("blk", "grp")),
            P(None, ("blk", "grp")),
        ),
        check_vma=False,
    )
```

```python
import jax
import jax.numpy as jnp
from jax import lax
from jax.experimental import pallas as pl
from jax.experimental.pallas import tpu as pltpu
from jax.sharding import PartitionSpec as P

log_total = 20.0
loss_scale = 1.0 / 256.0
step_rate = 0.1

WIDTH = 300
PADW = 304
LANES = 384
ROWS = 1024
HALF = 128
TILE = 256
SHARE = 32
PACK = 40

f32 = jnp.float32
bf16 = jnp.bfloat16
VM = pl.BlockSpec(memory_space=pltpu.VMEM)
FAR = pl.BlockSpec(memory_space=pl.ANY)


def split(value):
    high = value.astype(bf16)
    return high, (value - high.astype(f32)).astype(bf16)


def dot(left, right):
    return jnp.dot(left, right, preferred_element_type=f32)


def call(name, body, out, operands, scratch=(), far=0, room=4, flops=1 << 32):
    specs = [FAR] * far + [VM] * (len(operands) - far)
    spaces = [pltpu.HBM] * far + [pltpu.VMEM] * (len(operands) - far)
    placed = [pltpu.with_memory_space_constraint(each, space) for each, space in zip(operands, spaces)]
    return pl.pallas_call(
        body,
        out_shape=out,
        in_specs=specs,
        out_specs=jax.tree.map(lambda _: VM, out),
        scratch_shapes=list(scratch),
        compiler_params=pltpu.CompilerParams(vmem_limit_bytes=room * 1024 * 1024),
        cost_estimate=pl.CostEstimate(flops=flops, bytes_accessed=1 << 10, transcendentals=0),
        name=name,
    )(*placed)


def near(*dims, of=f32):
    return pltpu.VMEM(dims, of)


def free(*dims, of=f32):
    return jax.ShapeDtypeStruct(dims, of)


def fetch(source, target, done):
    copy = pltpu.make_async_copy(source, target, done)
    copy.start()
    return copy


def count_tables(counts_ref, logs_ref, target_ref, weight_ref):
    for at in range(0, ROWS, TILE):
        base = logs_ref[at : at + TILE, :]
        for side in range(0, 2 * HALF, HALF):
            counts = counts_ref[at : at + TILE, side : side + HALF].astype(f32)
            target_ref[at : at + TILE, side : side + HALF] = jnp.log(jnp.maximum(counts, 1.0)) + base
            weight = loss_scale * (0.1 + 0.25 * jnp.sqrt(counts))
            weight_ref[at : at + TILE, side : side + HALF] = jnp.where(counts > 0.5, weight, 0.0)


def prep_body(
    row_hbm, counts_hbm, vecs_hbm, moment_hbm, row_sums_hbm, col_sums_hbm,
    hi_ref, lo_ref, turned_hi_ref, turned_lo_ref, logs_ref, target_ref, weight_ref, left_ref, right_ref,
    given_ref, row_ref, counts_ref, vecs_ref, moment_ref, row_sums_ref, col_sums_ref, done,
):
    get_row_sums = fetch(row_sums_hbm, row_sums_ref, done.at[4])
    get_counts = fetch(counts_hbm.at[0], counts_ref, done.at[0])
    get_rows = fetch(row_hbm, given_ref, done.at[1])
    get_vecs = fetch(vecs_hbm, vecs_ref, done.at[2])
    get_moment = fetch(moment_hbm, moment_ref, done.at[3])
    get_col_sums = fetch(col_sums_hbm, col_sums_ref, done.at[5])
    get_row_sums.wait()
    logs = log_total - jnp.log(row_sums_ref[...].astype(f32))
    logs_ref[...] = jnp.broadcast_to(logs, (HALF, ROWS)).T
    row_ref[WIDTH:, :] = jnp.zeros((LANES - WIDTH, ROWS), f32)
    get_counts.wait()
    count_tables(counts_ref, logs_ref, target_ref, weight_ref)
    get_rows.wait()
    row_ref[0:WIDTH, :] = given_ref[...]
    high, low = split(given_ref[...])
    hi_ref[...] = high
    lo_ref[...] = low
    for at in range(0, ROWS, TILE):
        high, low = split(row_ref[:, at : at + TILE].T)
        turned_hi_ref[at : at + TILE, :] = high
        turned_lo_ref[at : at + TILE, :] = low
    get_vecs.wait()
    get_moment.wait()
    get_col_sums.wait()
    for side, ref in enumerate((left_ref, right_ref)):
        lanes = slice(side * HALF, (side + 1) * HALF)
        ref[0:WIDTH, :] = vecs_ref[:, lanes]
        ref[WIDTH:PADW, :] = jnp.broadcast_to(jnp.log(col_sums_ref[:, lanes].astype(f32)), (PADW - WIDTH, HALF))
        ref[PADW : PADW + WIDTH, :] = moment_ref[:, lanes]
        ref[PADW + WIDTH :, :] = jnp.zeros((PADW - WIDTH, HALF), f32)


def shares_body(row_hbm, acc_hbm, vecs_ref, moment_ref, given_ref, block_ref, turned_ref, done):
    group = lax.axis_index("grp")
    lanes = pl.ds(pl.multiple_of((group >> 2) * 128, 128), 128)
    gets = [fetch(source.at[:, lanes], given_ref.at[at], done.at[at]) for at, source in enumerate((row_hbm, acc_hbm))]
    for at, ref in enumerate((vecs_ref, moment_ref)):
        gets[at].wait()
        block_ref[0:WIDTH, :] = given_ref[at]
        block_ref[WIDTH:, :] = jnp.zeros((LANES - WIDTH, 128), f32)
        turned_ref[...] = block_ref[...].T
        ref[...] = turned_ref[pl.ds(pl.multiple_of((group & 3) * SHARE, SHARE), SHARE), 0:WIDTH]


def split_columns(vecs, both_ref):
    inside = lax.broadcasted_iota(jnp.int32, (PADW, HALF), 0) < WIDTH
    high, low = split(jnp.where(inside, vecs, 0.0))
    both_ref[0:PADW, 0:HALF] = high
    both_ref[0:PADW, HALF:] = low
    both_ref[PADW:, :] = jnp.zeros((LANES - PADW, 2 * HALF), bf16)


def cells(col_logs, both_ref, turned_hi_ref, turned_lo_ref, target_ref, weight_ref, grad_ref, side):
    for at in range(0, ROWS, TILE):
        rows = slice(at, at + TILE)
        lanes = slice(side * HALF, (side + 1) * HALF)
        wide = dot(turned_hi_ref[rows, :], both_ref[...])
        scores = wide[:, :HALF] + wide[:, HALF:] + dot(turned_lo_ref[rows, :], both_ref[:, :HALF])
        residue = scores - (target_ref[rows, lanes] - col_logs)
        weight = weight_ref[rows, lanes]
        seen = weight * residue
        unseen = loss_scale / (1.0 + jnp.exp(-residue))
        high, low = split(jnp.where(weight > 0.0, seen, unseen))
        grad_ref[rows, :HALF] = high
        grad_ref[rows, HALF:] = low


def col_grads(hi_ref, lo_ref, grad_ref):
    wide = dot(hi_ref[...], grad_ref[...])
    return wide[:, :HALF] + wide[:, HALF:] + dot(lo_ref[...], grad_ref[:, :HALF])


def updated(vecs, moment, grad):
    new_moment = moment + grad * grad
    return vecs - step_rate * grad / jnp.sqrt(new_moment), new_moment


def first_visit_body(side, state_ref, turned_hi_ref, turned_lo_ref, hi_ref, lo_ref, target_ref, weight_ref, vecs_ref, moment_ref, grad_ref, both_ref):
    split_columns(state_ref[0:PADW, :], both_ref)
    cells(state_ref[WIDTH : WIDTH + 1, :], both_ref, turned_hi_ref, turned_lo_ref, target_ref, weight_ref, grad_ref, side)
    grad = col_grads(hi_ref, lo_ref, grad_ref)
    vecs, moment = updated(state_ref[0:WIDTH, :], state_ref[PADW : PADW + WIDTH, :], grad)
    vecs_ref[0:WIDTH, :] = vecs
    vecs_ref[WIDTH:, :] = state_ref[WIDTH:PADW, :]
    moment_ref[0:WIDTH, :] = moment
    moment_ref[WIDTH:, :] = jnp.zeros((PADW - WIDTH, HALF), f32)


def second_visit_body(side, vecs_ref, turned_hi_ref, turned_lo_ref, hi_ref, lo_ref, target_ref, weight_ref, out_ref, grad_ref, both_ref):
    split_columns(vecs_ref[...], both_ref)
    cells(vecs_ref[WIDTH : WIDTH + 1, :], both_ref, turned_hi_ref, turned_lo_ref, target_ref, weight_ref, grad_ref, side)
    out_ref[0:WIDTH, :] = col_grads(hi_ref, lo_ref, grad_ref)
    out_ref[WIDTH:, :] = jnp.zeros((PADW - WIDTH, HALF), f32)


def third_visit_body(side, whole_ref, sent_ref, turned_hi_ref, turned_lo_ref, hi_ref, lo_ref, target_ref, weight_ref, *refs):
    now_ref, vecs_ref, moment_ref, grad_ref, both_ref = refs[-5:]
    if side:
        moment_ref[0:PADW, :] = refs[0][...]
    at = side * 2 * PADW
    vecs, moment = updated(whole_ref[at : at + WIDTH, :], whole_ref[at + PADW : at + PADW + WIDTH, :], sent_ref[0:WIDTH, :])
    now_ref[0:WIDTH, :] = vecs
    now_ref[WIDTH:, :] = whole_ref[at + WIDTH : at + PADW, :]
    split_columns(now_ref[...], both_ref)
    cells(now_ref[WIDTH : WIDTH + 1, :], both_ref, turned_hi_ref, turned_lo_ref, target_ref, weight_ref, grad_ref, side)
    vecs, moment = updated(now_ref[0:WIDTH, :], moment, col_grads(hi_ref, lo_ref, grad_ref))
    vecs_ref[0:WIDTH, :] = vecs
    vecs_ref[WIDTH:, :] = now_ref[WIDTH:, :]
    moment_ref[side * PADW : side * PADW + WIDTH, :] = moment
    moment_ref[side * PADW + WIDTH : (side + 1) * PADW, :] = jnp.zeros((PADW - WIDTH, HALF), f32)


def last_update_body(vecs_a_ref, vecs_b_ref, moments_ref, col_grad_a_ref, grad_b_ref, hi_ref, lo_ref, new_ref, new_moment_ref):
    for side, vecs_ref in enumerate((vecs_a_ref, vecs_b_ref)):
        grad = col_grads(hi_ref, lo_ref, grad_b_ref) if side else col_grad_a_ref[...]
        vecs, moment = updated(vecs_ref[0:WIDTH, :], moments_ref[side * PADW : side * PADW + WIDTH, :], grad)
        new_ref[:, side * HALF : (side + 1) * HALF] = vecs
        new_moment_ref[:, side * HALF : (side + 1) * HALF] = moment


def spread(vecs_ref, high_ref, low_ref):
    main_high, main_low = split(vecs_ref[0:256, :])
    tail = vecs_ref[256:PADW, :]
    inside = lax.broadcasted_iota(jnp.int32, (PADW - 256, HALF), 0) < WIDTH - 256
    tail_high, tail_low = split(jnp.where(inside, tail, 0.0))
    gap = jnp.zeros((64 - (PADW - 256), HALF), bf16)
    places = ((high_ref, 0, main_high, tail_high), (high_ref, HALF, main_high, tail_high), (low_ref, 0, main_low, tail_low))
    for ref, at, main, rest in places:
        ref[0:256, at : at + HALF] = main
        for start in (256, 320):
            ref[start : start + PADW - 256, at : at + HALF] = rest
            ref[start + PADW - 256 : start + 64, at : at + HALF] = gap


def row_part(grad_ref, high_ref, low_ref, rows):
    by_columns = (((1,), (1,)), ((), ()))
    part = lax.dot_general(grad_ref[rows, :], high_ref[...], by_columns, preferred_element_type=f32)
    return part + lax.dot_general(grad_ref[rows, :HALF], low_ref[...], by_columns, preferred_element_type=f32)


SPREAD = [pltpu.VMEM((LANES, 2 * HALF), bf16), pltpu.VMEM((LANES, HALF), bf16)]


def tables_body(turn, counts_hbm, logs_ref, after_ref, *refs):
    packs = len(refs) - 4 - (1 if len(refs) > 4 else 0)
    target_ref, weight_ref, counts_ref, done = refs[-4:]
    get_counts = fetch(counts_hbm.at[turn + 1], counts_ref, done)
    for at in range(packs):
        refs[packs][at * PADW : (at + 1) * PADW, :] = refs[at][...]
    get_counts.wait()
    count_tables(counts_ref, logs_ref, target_ref, weight_ref)


def rows_body(more, vecs_a_ref, vecs_b_ref, grad_a_ref, grad_b_ref, *refs):
    before_ref = refs[0] if more else None
    total_ref, high_a_ref, low_a_ref, high_b_ref, low_b_ref = refs[-5:]
    spread(vecs_a_ref, high_a_ref, low_a_ref)
    spread(vecs_b_ref, high_b_ref, low_b_ref)
    for at in range(0, ROWS, TILE):
        rows = slice(at, at + TILE)
        part = row_part(grad_a_ref, high_a_ref, low_a_ref, rows) + row_part(grad_b_ref, high_b_ref, low_b_ref, rows)
        total_ref[rows, :] = before_ref[rows, :] + part if more else part


def last_half(side, vecs_ref, turned_hi_ref, turned_lo_ref, target_ref, weight_ref, before_ref, grad_ref, total_ref, both_ref, high_ref, low_ref):
    split_columns(vecs_ref[0:PADW, :], both_ref)
    cells(vecs_ref[WIDTH : WIDTH + 1, :], both_ref, turned_hi_ref, turned_lo_ref, target_ref, weight_ref, grad_ref, side)
    spread(vecs_ref, high_ref, low_ref)
    for at in range(0, ROWS, TILE):
        rows = slice(at, at + TILE)
        total_ref[rows, :] = before_ref[rows, :] + row_part(grad_ref, high_ref, low_ref, rows)


def last_first_body(vecs_ref, turned_hi_ref, turned_lo_ref, target_ref, weight_ref, before_ref, hi_ref, lo_ref, total_ref, col_grad_ref, grad_ref, *scratch):
    last_half(0, vecs_ref, turned_hi_ref, turned_lo_ref, target_ref, weight_ref, before_ref, grad_ref, total_ref, *scratch)
    col_grad_ref[...] = col_grads(hi_ref, lo_ref, grad_ref)


def last_body(side, vecs_ref, turned_hi_ref, turned_lo_ref, target_ref, weight_ref, before_ref, grad_ref, keep_ref, send_ref, total_ref, *scratch):
    last_half(side, vecs_ref, turned_hi_ref, turned_lo_ref, target_ref, weight_ref, before_ref, grad_ref, total_ref, *scratch)
    core = lax.axis_index("grp") & 1
    left = lax.broadcasted_iota(jnp.int32, (8, 128), 1) < 64
    for ref, half in ((keep_ref, core), (send_ref, 1 - core)):
        for slot in range(16):
            base = pl.multiple_of(slot * 2 * SHARE + half * SHARE, SHARE)
            block = total_ref[pl.ds(base, SHARE), :]
            ref[slot * PACK : slot * PACK + SHARE, :] = block[:, :256]
            for pair in range(2):
                upper = block[pair * 16 : pair * 16 + 8, 256:]
                lower = block[pair * 16 + 8 : pair * 16 + 16, 256:]
                ref[slot * PACK + SHARE : (slot + 1) * PACK, pair * 128 : (pair + 1) * 128] = jnp.where(left, upper, lower)


def sum_body(new_ref, new_moment_ref, keep_ref, got_ref, out_ref):
    for slot in range(16):
        rows = slice(slot * PACK, (slot + 1) * PACK)
        out_ref[slot] = keep_ref[rows, :] + got_ref[rows, :]


def finish_body(parts_ref, vecs_ref, moment_ref, new_ref, new_moment_ref, grad_ref):
    total = parts_ref[0]
    for at in range(1, parts_ref.shape[0]):
        total = total + parts_ref[at]
    grad_ref[:, :256] = total[0:SHARE, :]
    for group in range(4):
        rest = total[SHARE:PACK, (group // 2) * 128 : (group // 2 + 1) * 128]
        if group % 2:
            rest = pltpu.roll(rest, 64, 1)
        grad_ref[group * 8 : (group + 1) * 8, 256:] = rest
    vecs, moment = updated(vecs_ref[...], moment_ref[...], grad_ref[:, :WIDTH])
    new_ref[...] = vecs
    new_moment_ref[...] = moment


def shifted(value, steps=1):
    count = lax.axis_size("blk")
    return lax.ppermute(value, "blk", [(source, (source + steps) % count) for source in range(count)])


def swapped(value, bit):
    count = lax.axis_size("grp")
    return lax.ppermute(value, "grp", [(source, source ^ bit) for source in range(count)])


def shards(counts, row_sums, col_sums, row_emb, row_acc, col_emb, col_acc):
    cell_half = near(ROWS, 2 * HALF, of=bf16)
    table = near(ROWS, 2 * HALF)
    both = pltpu.VMEM((LANES, 2 * HALF), bf16)

    hi, lo, turned_hi, turned_lo, row_logs, target, weight, *states = call(
        "prep",
        prep_body,
        (near(WIDTH, ROWS, of=bf16),) * 2 + (near(ROWS, LANES, of=bf16),) * 2 + (near(ROWS, HALF), table, table) + (near(2 * PADW, HALF),) * 2,
        (row_emb, counts, col_emb, col_acc, row_sums.reshape(1, ROWS), col_sums.reshape(1, 2 * HALF)),
        [
            pltpu.VMEM((WIDTH, ROWS), f32),
            pltpu.VMEM((LANES, ROWS), f32),
            pltpu.VMEM((ROWS, 2 * HALF), bf16),
            pltpu.VMEM((WIDTH, 2 * HALF), f32),
            pltpu.VMEM((WIDTH, 2 * HALF), f32),
            pltpu.VMEM((1, ROWS), jnp.int32),
            pltpu.VMEM((1, 2 * HALF), jnp.int32),
            pltpu.SemaphoreType.DMA((6,)),
        ],
        far=6,
        room=6,
    )

    rows = (turned_hi, turned_lo, hi, lo)

    def beside(turn, vecs, grads, packs, *more):
        packed = (near(len(packs) * PADW, HALF),) if packs else ()
        *packed, target, weight = call(
            "tables",
            lambda *refs: tables_body(turn, *refs),
            (*packed, table, table),
            (counts, row_logs, grads[1], *packs),
            [pltpu.VMEM((ROWS, 2 * HALF), bf16), pltpu.SemaphoreType.DMA(())],
            far=1,
            flops=1 << 20,
        )
        total = call(
            "rows",
            lambda *refs: rows_body(turn > 0, *refs),
            near(ROWS, LANES),
            (*vecs, *grads, *more),
            SPREAD * 2,
            flops=1 << 20,
        )
        return (*packed, total, target, weight)

    near_vecs = near(PADW, HALF)
    vecs, moments, grads = [None] * 2, [None] * 2, [None] * 2
    for side in range(2):
        vecs[side], moments[side], grads[side] = call(
            "first_visit",
            lambda *refs, side=side: first_visit_body(side, *refs),
            (near_vecs, near_vecs, cell_half),
            (states[side], *rows, target, weight),
            [both],
        )
    whole, total, target, weight = beside(0, states, grads, (vecs[0], moments[0], vecs[1], moments[1]))
    whole = shifted(whole, 2)
    vecs = [shifted(each) for each in vecs]

    sent, grads = [None] * 2, [None] * 2
    for side in range(2):
        sent[side], grads[side] = call(
            "second_visit",
            lambda *refs, side=side: second_visit_body(side, *refs),
            (near_vecs, cell_half),
            (vecs[side], *rows, target, weight),
            [both],
        )
        sent[side] = shifted(sent[side])
    total, target, weight = beside(1, vecs, grads, (), total)

    now, vecs, grads, moments = [None] * 2, [None] * 2, [None] * 2, ()
    for side in range(2):
        now[side], vecs[side], *moments, grads[side] = call(
            "third_visit",
            lambda *refs, side=side: third_visit_body(side, *refs),
            (near_vecs, near_vecs, near((1 + side) * PADW, HALF), cell_half),
            (whole, sent[side], *rows, target, weight, *moments),
            [both],
        )
        vecs[side] = shifted(vecs[side])
    moments = shifted(moments[0])
    total, target, weight = beside(2, now, grads, (), total)

    part, col_grad_a = call(
        "last_first",
        last_first_body,
        (near(ROWS, LANES), near(WIDTH, HALF)),
        (vecs[0], turned_hi, turned_lo, target, weight, total, hi, lo),
        [pltpu.VMEM((ROWS, 2 * HALF), bf16), both] + SPREAD,
    )
    grad_b, keep, send = call(
        "last_second",
        lambda *refs: last_body(1, *refs),
        (cell_half, near(16 * PACK, 256), near(16 * PACK, 256)),
        (vecs[1], turned_hi, turned_lo, target, weight, part),
        [pltpu.VMEM((ROWS, LANES), f32), both] + SPREAD,
        room=6,
    )
    new_col_emb, new_col_acc = call(
        "last_update",
        last_update_body,
        (free(WIDTH, 2 * HALF), free(WIDTH, 2 * HALF)),
        (vecs[0], vecs[1], moments, col_grad_a, grad_b, hi, lo),
        flops=1 << 32,
    )

    own_vecs, own_moment = call(
        "shares",
        shares_body,
        (near(SHARE, WIDTH), near(SHARE, WIDTH)),
        (row_emb, row_acc),
        [pltpu.VMEM((2, WIDTH, 128), f32), pltpu.VMEM((LANES, 128), f32), pltpu.VMEM((128, LANES), f32), pltpu.SemaphoreType.DMA((2,))],
        far=2,
    )
    got = swapped(send, 1)
    share = call("sum", sum_body, near(16, PACK, 256), (new_col_emb, new_col_acc, keep, got), far=2)
    chips = [[2 * chip + core for chip in range(16)] for core in range(2)]
    parts = lax.all_to_all(share, "grp", 0, 0, axis_index_groups=chips)

    new_rows, new_row_moment = call(
        "finish",
        finish_body,
        (free(SHARE, WIDTH), free(SHARE, WIDTH)),
        (parts, own_vecs, own_moment),
        [pltpu.VMEM((SHARE, LANES), f32)],
    )
    return (new_rows.T, new_row_moment.T, new_col_emb, new_col_acc)


def solution(mesh):
    return jax.shard_map(
        shards,
        mesh=mesh,
        in_specs=(
            P(None, "blk", "grp"),
            P("blk"),
            P(("blk", "grp")),
            P(None, "blk"),
            P(None, "blk"),
            P(None, ("blk", "grp")),
            P(None, ("blk", "grp")),
        ),
        out_specs=(
            P(None, ("blk", "grp")),
            P(None, ("blk", "grp")),
            P(None, ("blk", "grp")),
            P(None, ("blk", "grp")),
        ),
        check_vma=False,
    )
```

```python
import jax
import jax.numpy as jnp
from jax import lax
from jax.experimental import pallas as pl
from jax.experimental.pallas import tpu as pltpu
from jax.sharding import PartitionSpec as P

log_total = 20.0
loss_scale = 1.0 / 256.0
step_rate = 0.1

WIDTH = 300
PADW = 304
LANES = 384
ROWS = 1024
HALF = 128
TILE = 256
SHARE = 32
PACK = 40

f32 = jnp.float32
bf16 = jnp.bfloat16
VM = pl.BlockSpec(memory_space=pltpu.VMEM)
FAR = pl.BlockSpec(memory_space=pl.ANY)


def split(value):
    high = value.astype(bf16)
    return high, (value - high.astype(f32)).astype(bf16)


def dot(left, right):
    return jnp.dot(left, right, preferred_element_type=f32)


def call(name, body, out, operands, scratch=(), far=0, room=4, flops=1 << 32):
    specs = [FAR] * far + [VM] * (len(operands) - far)
    spaces = [pltpu.HBM] * far + [pltpu.VMEM] * (len(operands) - far)
    placed = [pltpu.with_memory_space_constraint(each, space) for each, space in zip(operands, spaces)]
    return pl.pallas_call(
        body,
        out_shape=out,
        in_specs=specs,
        out_specs=jax.tree.map(lambda _: VM, out),
        scratch_shapes=list(scratch),
        compiler_params=pltpu.CompilerParams(vmem_limit_bytes=room * 1024 * 1024),
        cost_estimate=pl.CostEstimate(flops=flops, bytes_accessed=1 << 10, transcendentals=0),
        name=name,
    )(*placed)


def near(*dims, of=f32):
    return pltpu.VMEM(dims, of)


def remote(*dims, of=f32):
    return pltpu.HBM(dims, of)


def free(*dims, of=f32):
    return jax.ShapeDtypeStruct(dims, of)


def fetch(source, target, done):
    copy = pltpu.make_async_copy(source, target, done)
    copy.start()
    return copy


def count_tables(counts_ref, logs_ref, target_ref, weight_ref):
    for at in range(0, ROWS, TILE):
        base = logs_ref[at : at + TILE, :]
        for side in range(0, 2 * HALF, HALF):
            counts = counts_ref[at : at + TILE, side : side + HALF].astype(f32)
            target_ref[at : at + TILE, side : side + HALF] = jnp.log(jnp.maximum(counts, 1.0)) + base
            weight = loss_scale * (0.1 + 0.25 * jnp.sqrt(counts))
            weight_ref[at : at + TILE, side : side + HALF] = jnp.where(counts > 0.5, weight, 0.0)


def prep_body(
    row_hbm, counts_hbm, vecs_hbm, moment_hbm, row_sums_hbm, col_sums_hbm,
    hi_ref, lo_ref, turned_hi_ref, turned_lo_ref, logs_ref, target_ref, weight_ref, left_ref, right_ref,
    given_ref, row_ref, counts_ref, vecs_ref, moment_ref, row_sums_ref, col_sums_ref, done,
):
    get_row_sums = fetch(row_sums_hbm, row_sums_ref, done.at[4])
    get_counts = fetch(counts_hbm.at[0], counts_ref, done.at[0])
    get_rows = fetch(row_hbm, given_ref, done.at[1])
    get_vecs = fetch(vecs_hbm, vecs_ref, done.at[2])
    get_moment = fetch(moment_hbm, moment_ref, done.at[3])
    get_col_sums = fetch(col_sums_hbm, col_sums_ref, done.at[5])
    get_row_sums.wait()
    logs = log_total - jnp.log(row_sums_ref[...].astype(f32))
    logs_ref[...] = jnp.broadcast_to(logs, (HALF, ROWS)).T
    row_ref[WIDTH:, :] = jnp.zeros((LANES - WIDTH, ROWS), f32)
    get_counts.wait()
    count_tables(counts_ref, logs_ref, target_ref, weight_ref)
    get_rows.wait()
    row_ref[0:WIDTH, :] = given_ref[...]
    high, low = split(given_ref[...])
    hi_ref[...] = high
    lo_ref[...] = low
    for at in range(0, ROWS, TILE):
        high, low = split(row_ref[:, at : at + TILE].T)
        turned_hi_ref[at : at + TILE, :] = high
        turned_lo_ref[at : at + TILE, :] = low
    get_vecs.wait()
    get_moment.wait()
    get_col_sums.wait()
    for side, ref in enumerate((left_ref, right_ref)):
        lanes = slice(side * HALF, (side + 1) * HALF)
        ref[0:WIDTH, :] = vecs_ref[:, lanes]
        ref[WIDTH:PADW, :] = jnp.broadcast_to(jnp.log(col_sums_ref[:, lanes].astype(f32)), (PADW - WIDTH, HALF))
        ref[PADW : PADW + WIDTH, :] = moment_ref[:, lanes]
        ref[PADW + WIDTH :, :] = jnp.zeros((PADW - WIDTH, HALF), f32)


def shares_body(row_hbm, acc_hbm, vecs_ref, moment_ref, given_ref, block_ref, turned_ref, done):
    group = lax.axis_index("grp")
    lanes = pl.ds(pl.multiple_of((group >> 2) * 128, 128), 128)
    gets = [fetch(source.at[:, lanes], given_ref.at[at], done.at[at]) for at, source in enumerate((row_hbm, acc_hbm))]
    for at, ref in enumerate((vecs_ref, moment_ref)):
        gets[at].wait()
        block_ref[0:WIDTH, :] = given_ref[at]
        block_ref[WIDTH:, :] = jnp.zeros((LANES - WIDTH, 128), f32)
        turned_ref[...] = block_ref[...].T
        ref[...] = turned_ref[pl.ds(pl.multiple_of((group & 3) * SHARE, SHARE), SHARE), 0:WIDTH]


def split_columns(vecs, both_ref):
    inside = lax.broadcasted_iota(jnp.int32, (PADW, HALF), 0) < WIDTH
    high, low = split(jnp.where(inside, vecs, 0.0))
    both_ref[0:PADW, 0:HALF] = high
    both_ref[0:PADW, HALF:] = low
    both_ref[PADW:, :] = jnp.zeros((LANES - PADW, 2 * HALF), bf16)


def cells(col_logs, both_ref, turned_hi_ref, turned_lo_ref, target_ref, weight_ref, grad_ref, side):
    for at in range(0, ROWS, TILE):
        rows = slice(at, at + TILE)
        lanes = slice(side * HALF, (side + 1) * HALF)
        wide = dot(turned_hi_ref[rows, :], both_ref[...])
        scores = wide[:, :HALF] + wide[:, HALF:] + dot(turned_lo_ref[rows, :], both_ref[:, :HALF])
        residue = scores - (target_ref[rows, lanes] - col_logs)
        weight = weight_ref[rows, lanes]
        seen = weight * residue
        unseen = loss_scale / (1.0 + jnp.exp(-residue))
        high, low = split(jnp.where(weight > 0.0, seen, unseen))
        grad_ref[rows, :HALF] = high
        grad_ref[rows, HALF:] = low


def col_grads(hi_ref, lo_ref, grad_ref):
    wide = dot(hi_ref[...], grad_ref[...])
    return wide[:, :HALF] + wide[:, HALF:] + dot(lo_ref[...], grad_ref[:, :HALF])


def updated(vecs, moment, grad):
    new_moment = moment + grad * grad
    return vecs - step_rate * grad / jnp.sqrt(new_moment), new_moment


def first_visit_body(side, state_ref, turned_hi_ref, turned_lo_ref, hi_ref, lo_ref, target_ref, weight_ref, vecs_ref, moment_ref, grad_ref, both_ref):
    split_columns(state_ref[0:PADW, :], both_ref)
    cells(state_ref[WIDTH : WIDTH + 1, :], both_ref, turned_hi_ref, turned_lo_ref, target_ref, weight_ref, grad_ref, side)
    grad = col_grads(hi_ref, lo_ref, grad_ref)
    vecs, moment = updated(state_ref[0:WIDTH, :], state_ref[PADW : PADW + WIDTH, :], grad)
    vecs_ref[0:WIDTH, :] = vecs
    vecs_ref[WIDTH:, :] = state_ref[WIDTH:PADW, :]
    moment_ref[0:WIDTH, :] = moment
    moment_ref[WIDTH:, :] = jnp.zeros((PADW - WIDTH, HALF), f32)


def second_visit_body(side, vecs_ref, turned_hi_ref, turned_lo_ref, hi_ref, lo_ref, target_ref, weight_ref, out_ref, grad_ref, both_ref):
    split_columns(vecs_ref[...], both_ref)
    cells(vecs_ref[WIDTH : WIDTH + 1, :], both_ref, turned_hi_ref, turned_lo_ref, target_ref, weight_ref, grad_ref, side)
    out_ref[0:WIDTH, :] = col_grads(hi_ref, lo_ref, grad_ref)
    out_ref[WIDTH:, :] = jnp.zeros((PADW - WIDTH, HALF), f32)


def third_visit_body(side, whole_ref, sent_ref, turned_hi_ref, turned_lo_ref, hi_ref, lo_ref, target_ref, weight_ref, *refs):
    now_ref, vecs_ref, moment_ref, grad_ref, both_ref = refs[-5:]
    if side:
        moment_ref[0:PADW, :] = refs[0][...]
    at = side * 2 * PADW
    vecs, moment = updated(whole_ref[at : at + WIDTH, :], whole_ref[at + PADW : at + PADW + WIDTH, :], sent_ref[0:WIDTH, :])
    now_ref[0:WIDTH, :] = vecs
    now_ref[WIDTH:, :] = whole_ref[at + WIDTH : at + PADW, :]
    split_columns(now_ref[...], both_ref)
    cells(now_ref[WIDTH : WIDTH + 1, :], both_ref, turned_hi_ref, turned_lo_ref, target_ref, weight_ref, grad_ref, side)
    vecs, moment = updated(now_ref[0:WIDTH, :], moment, col_grads(hi_ref, lo_ref, grad_ref))
    vecs_ref[0:WIDTH, :] = vecs
    vecs_ref[WIDTH:, :] = now_ref[WIDTH:, :]
    moment_ref[side * PADW : side * PADW + WIDTH, :] = moment
    moment_ref[side * PADW + WIDTH : (side + 1) * PADW, :] = jnp.zeros((PADW - WIDTH, HALF), f32)


def last_update_body(kept_a_hbm, kept_b_hbm, col_grad_a_hbm, col_grad_b_hbm, moments_ref, new_ref, new_moment_ref, *scratch):
    *refs, done = scratch
    sources = (kept_a_hbm, kept_b_hbm, col_grad_a_hbm, col_grad_b_hbm)
    gets = [fetch(source, ref, done.at[at]) for at, (source, ref) in enumerate(zip(sources, refs))]
    for get in gets:
        get.wait()
    for side in range(2):
        vecs, moment = updated(refs[side][0:WIDTH, :], moments_ref[side * PADW : side * PADW + WIDTH, :], refs[2 + side][0:WIDTH, :])
        new_ref[:, side * HALF : (side + 1) * HALF] = vecs
        new_moment_ref[:, side * HALF : (side + 1) * HALF] = moment


def spread(vecs_ref, high_ref, low_ref):
    main_high, main_low = split(vecs_ref[0:256, :])
    tail = vecs_ref[256:PADW, :]
    inside = lax.broadcasted_iota(jnp.int32, (PADW - 256, HALF), 0) < WIDTH - 256
    tail_high, tail_low = split(jnp.where(inside, tail, 0.0))
    gap = jnp.zeros((64 - (PADW - 256), HALF), bf16)
    places = ((high_ref, 0, main_high, tail_high), (high_ref, HALF, main_high, tail_high), (low_ref, 0, main_low, tail_low))
    for ref, at, main, rest in places:
        ref[0:256, at : at + HALF] = main
        for start in (256, 320):
            ref[start : start + PADW - 256, at : at + HALF] = rest
            ref[start + PADW - 256 : start + 64, at : at + HALF] = gap


def row_part(grad_ref, high_ref, low_ref, rows):
    by_columns = (((1,), (1,)), ((), ()))
    part = lax.dot_general(grad_ref[rows, :], high_ref[...], by_columns, preferred_element_type=f32)
    return part + lax.dot_general(grad_ref[rows, :HALF], low_ref[...], by_columns, preferred_element_type=f32)


SPREAD = [pltpu.VMEM((LANES, 2 * HALF), bf16), pltpu.VMEM((LANES, HALF), bf16)]


def pack_body(*refs):
    for at, ref in enumerate(refs[:-1]):
        refs[-1][at * PADW : (at + 1) * PADW, :] = ref[...]


def tables_body(turn, counts_hbm, logs_ref, after_ref, target_ref, weight_ref, counts_ref, done):
    get_counts = fetch(counts_hbm.at[turn + 1], counts_ref, done)
    get_counts.wait()
    count_tables(counts_ref, logs_ref, target_ref, weight_ref)


def rows_body(more, vecs_a_ref, vecs_b_ref, grad_a_ref, grad_b_ref, *refs):
    before_ref = refs[0] if more else None
    total_ref, high_a_ref, low_a_ref, high_b_ref, low_b_ref = refs[-5:]
    spread(vecs_a_ref, high_a_ref, low_a_ref)
    spread(vecs_b_ref, high_b_ref, low_b_ref)
    for at in range(0, ROWS, TILE):
        rows = slice(at, at + TILE)
        part = row_part(grad_a_ref, high_a_ref, low_a_ref, rows) + row_part(grad_b_ref, high_b_ref, low_b_ref, rows)
        total_ref[rows, :] = before_ref[rows, :] + part if more else part


def last_half(side, vecs_ref, turned_hi_ref, turned_lo_ref, target_ref, weight_ref, before_ref, grad_ref, total_ref, both_ref, high_ref, low_ref):
    split_columns(vecs_ref[0:PADW, :], both_ref)
    cells(vecs_ref[WIDTH : WIDTH + 1, :], both_ref, turned_hi_ref, turned_lo_ref, target_ref, weight_ref, grad_ref, side)
    spread(vecs_ref, high_ref, low_ref)
    for at in range(0, ROWS, TILE):
        rows = slice(at, at + TILE)
        total_ref[rows, :] = before_ref[rows, :] + row_part(grad_ref, high_ref, low_ref, rows)


def keep_columns(vecs_ref, hi_ref, lo_ref, grad_ref, kept_ref, col_grad_ref):
    kept_ref[...] = vecs_ref[...]
    col_grad_ref[0:WIDTH, :] = col_grads(hi_ref, lo_ref, grad_ref)
    col_grad_ref[WIDTH:, :] = jnp.zeros((PADW - WIDTH, HALF), f32)


def last_first_body(vecs_ref, turned_hi_ref, turned_lo_ref, target_ref, weight_ref, before_ref, hi_ref, lo_ref, total_ref, kept_ref, col_grad_ref, grad_ref, *scratch):
    last_half(0, vecs_ref, turned_hi_ref, turned_lo_ref, target_ref, weight_ref, before_ref, grad_ref, total_ref, *scratch)
    keep_columns(vecs_ref, hi_ref, lo_ref, grad_ref, kept_ref, col_grad_ref)


def last_body(side, vecs_ref, turned_hi_ref, turned_lo_ref, target_ref, weight_ref, before_ref, grad_ref, keep_ref, send_ref, total_ref, *scratch):
    last_half(side, vecs_ref, turned_hi_ref, turned_lo_ref, target_ref, weight_ref, before_ref, grad_ref, total_ref, *scratch)
    core = lax.axis_index("grp") & 1
    left = lax.broadcasted_iota(jnp.int32, (8, 128), 1) < 64
    for ref, half in ((keep_ref, core), (send_ref, 1 - core)):
        for slot in range(16):
            base = pl.multiple_of(slot * 2 * SHARE + half * SHARE, SHARE)
            block = total_ref[pl.ds(base, SHARE), :]
            ref[slot * PACK : slot * PACK + SHARE, :] = block[:, :256]
            for pair in range(2):
                upper = block[pair * 16 : pair * 16 + 8, 256:]
                lower = block[pair * 16 + 8 : pair * 16 + 16, 256:]
                ref[slot * PACK + SHARE : (slot + 1) * PACK, pair * 128 : (pair + 1) * 128] = jnp.where(left, upper, lower)


def sum_body(kept_ref, keep_ref, got_ref, out_ref):
    for slot in range(16):
        rows = slice(slot * PACK, (slot + 1) * PACK)
        out_ref[slot] = keep_ref[rows, :] + got_ref[rows, :]


def finish_body(parts_ref, vecs_ref, moment_ref, new_ref, new_moment_ref, grad_ref):
    total = parts_ref[0]
    for at in range(1, parts_ref.shape[0]):
        total = total + parts_ref[at]
    grad_ref[:, :256] = total[0:SHARE, :]
    for group in range(4):
        rest = total[SHARE:PACK, (group // 2) * 128 : (group // 2 + 1) * 128]
        if group % 2:
            rest = pltpu.roll(rest, 64, 1)
        grad_ref[group * 8 : (group + 1) * 8, 256:] = rest
    vecs, moment = updated(vecs_ref[...], moment_ref[...], grad_ref[:, :WIDTH])
    new_ref[...] = vecs
    new_moment_ref[...] = moment


def shifted(value, steps=1):
    count = lax.axis_size("blk")
    return lax.ppermute(value, "blk", [(source, (source + steps) % count) for source in range(count)])


def swapped(value, bit):
    count = lax.axis_size("grp")
    return lax.ppermute(value, "grp", [(source, source ^ bit) for source in range(count)])


def shards(counts, row_sums, col_sums, row_emb, row_acc, col_emb, col_acc):
    cell_half = near(ROWS, 2 * HALF, of=bf16)
    table = near(ROWS, 2 * HALF)
    both = pltpu.VMEM((LANES, 2 * HALF), bf16)

    hi, lo, turned_hi, turned_lo, row_logs, target, weight, *states = call(
        "prep",
        prep_body,
        (near(WIDTH, ROWS, of=bf16),) * 2 + (near(ROWS, LANES, of=bf16),) * 2 + (near(ROWS, HALF), table, table) + (near(2 * PADW, HALF),) * 2,
        (row_emb, counts, col_emb, col_acc, row_sums.reshape(1, ROWS), col_sums.reshape(1, 2 * HALF)),
        [
            pltpu.VMEM((WIDTH, ROWS), f32),
            pltpu.VMEM((LANES, ROWS), f32),
            pltpu.VMEM((ROWS, 2 * HALF), bf16),
            pltpu.VMEM((WIDTH, 2 * HALF), f32),
            pltpu.VMEM((WIDTH, 2 * HALF), f32),
            pltpu.VMEM((1, ROWS), jnp.int32),
            pltpu.VMEM((1, 2 * HALF), jnp.int32),
            pltpu.SemaphoreType.DMA((6,)),
        ],
        far=6,
        room=6,
    )

    rows = (turned_hi, turned_lo, hi, lo)

    def beside(turn, vecs, grads, after, *more):
        target, weight = call(
            "tables",
            lambda *refs: tables_body(turn, *refs),
            (table, table),
            (counts, row_logs, after),
            [pltpu.VMEM((ROWS, 2 * HALF), bf16), pltpu.SemaphoreType.DMA(())],
            far=1,
            flops=1 << 20,
        )
        total = call(
            "rows",
            lambda *refs: rows_body(turn > 0, *refs),
            near(ROWS, LANES),
            (*vecs, *grads, *more),
            SPREAD * 2,
            flops=1 << 20,
        )
        return total, target, weight

    near_vecs = near(PADW, HALF)
    vecs, moments, grads = [None] * 2, [None] * 2, [None] * 2
    for side in range(2):
        vecs[side], moments[side], grads[side] = call(
            "first_visit",
            lambda *refs, side=side: first_visit_body(side, *refs),
            (near_vecs, near_vecs, cell_half),
            (states[side], *rows, target, weight),
            [both],
        )
    whole = call("pack", pack_body, near(4 * PADW, HALF), (vecs[0], moments[0], vecs[1], moments[1]), flops=1 << 20)
    total, target, weight = beside(0, states, grads, whole)
    whole = shifted(whole, 2)
    vecs = [shifted(each) for each in vecs]

    sent, grads = [None] * 2, [None] * 2
    for side in range(2):
        sent[side], grads[side] = call(
            "second_visit",
            lambda *refs, side=side: second_visit_body(side, *refs),
            (near_vecs, cell_half),
            (vecs[side], *rows, target, weight),
            [both],
        )
        sent[side] = shifted(sent[side])
    total, target, weight = beside(1, vecs, grads, grads[1], total)

    now, vecs, grads, moments = [None] * 2, [None] * 2, [None] * 2, ()
    for side in range(2):
        now[side], vecs[side], *moments, grads[side] = call(
            "third_visit",
            lambda *refs, side=side: third_visit_body(side, *refs),
            (near_vecs, near_vecs, near((1 + side) * PADW, HALF), cell_half),
            (whole, sent[side], *rows, target, weight, *moments),
            [both],
        )
        vecs[side] = shifted(vecs[side])
    moments = shifted(moments[0])
    total, target, weight = beside(2, now, grads, grads[1], total)

    part, kept_a, col_grad_a = call(
        "last_first",
        last_first_body,
        (near(ROWS, LANES), remote(PADW, HALF), remote(PADW, HALF)),
        (vecs[0], turned_hi, turned_lo, target, weight, total, hi, lo),
        [pltpu.VMEM((ROWS, 2 * HALF), bf16), both] + SPREAD,
    )
    grad_b, keep, send = call(
        "last_second",
        lambda *refs: last_body(1, *refs),
        (cell_half, near(16 * PACK, 256), near(16 * PACK, 256)),
        (vecs[1], turned_hi, turned_lo, target, weight, part),
        [pltpu.VMEM((ROWS, LANES), f32), both] + SPREAD,
        room=6,
    )
    kept_b, col_grad_b = call(
        "last_columns",
        keep_columns,
        (remote(PADW, HALF), remote(PADW, HALF)),
        (vecs[1], hi, lo, grad_b),
        flops=1 << 20,
    )
    small = pltpu.VMEM((PADW, HALF), f32)
    new_col_emb, new_col_acc = call(
        "last_update",
        last_update_body,
        (free(WIDTH, 2 * HALF), free(WIDTH, 2 * HALF)),
        (kept_a, kept_b, col_grad_a, col_grad_b, moments),
        [small] * 4 + [pltpu.SemaphoreType.DMA((4,))],
        far=4,
        flops=1 << 20,
    )

    own_vecs, own_moment = call(
        "shares",
        shares_body,
        (near(SHARE, WIDTH), near(SHARE, WIDTH)),
        (row_emb, row_acc),
        [pltpu.VMEM((2, WIDTH, 128), f32), pltpu.VMEM((LANES, 128), f32), pltpu.VMEM((128, LANES), f32), pltpu.SemaphoreType.DMA((2,))],
        far=2,
    )
    got = swapped(send, 1)
    share = call("sum", sum_body, near(16, PACK, 256), (kept_b, keep, got), far=1)
    chips = [[2 * chip + core for chip in range(16)] for core in range(2)]
    parts = lax.all_to_all(share, "grp", 0, 0, axis_index_groups=chips)

    new_rows, new_row_moment = call(
        "finish",
        finish_body,
        (free(SHARE, WIDTH), free(SHARE, WIDTH)),
        (parts, own_vecs, own_moment),
        [pltpu.VMEM((SHARE, LANES), f32)],
    )
    return (new_rows.T, new_row_moment.T, new_col_emb, new_col_acc)


def solution(mesh):
    return jax.shard_map(
        shards,
        mesh=mesh,
        in_specs=(
            P(None, "blk", "grp"),
            P("blk"),
            P(("blk", "grp")),
            P(None, "blk"),
            P(None, "blk"),
            P(None, ("blk", "grp")),
            P(None, ("blk", "grp")),
        ),
        out_specs=(
            P(None, ("blk", "grp")),
            P(None, ("blk", "grp")),
            P(None, ("blk", "grp")),
            P(None, ("blk", "grp")),
        ),
        check_vma=False,
    )
```

```python
import jax
import jax.numpy as jnp
from jax import lax
from jax.experimental import pallas as pl
from jax.experimental.pallas import tpu as pltpu
from jax.sharding import PartitionSpec as P

log_total = 20.0
loss_scale = 1.0 / 256.0
step_rate = 0.1

WIDTH = 300
PADW = 304
LANES = 384
ROWS = 1024
HALF = 128
TILE = 256
SHARE = 32
PACK = 40

f32 = jnp.float32
bf16 = jnp.bfloat16
VM = pl.BlockSpec(memory_space=pltpu.VMEM)
FAR = pl.BlockSpec(memory_space=pl.ANY)


def split(value):
    high = value.astype(bf16)
    return high, (value - high.astype(f32)).astype(bf16)


def dot(left, right):
    return jnp.dot(left, right, preferred_element_type=f32)


def call(name, body, out, operands, scratch=(), far=0, room=4, flops=1 << 32):
    specs = [FAR] * far + [VM] * (len(operands) - far)
    spaces = [pltpu.HBM] * far + [pltpu.VMEM] * (len(operands) - far)
    placed = [pltpu.with_memory_space_constraint(each, space) for each, space in zip(operands, spaces)]
    return pl.pallas_call(
        body,
        out_shape=out,
        in_specs=specs,
        out_specs=jax.tree.map(lambda _: VM, out),
        scratch_shapes=list(scratch),
        compiler_params=pltpu.CompilerParams(vmem_limit_bytes=room * 1024 * 1024),
        cost_estimate=pl.CostEstimate(flops=flops, bytes_accessed=1 << 10, transcendentals=0),
        name=name,
    )(*placed)


def near(*dims, of=f32):
    return pltpu.VMEM(dims, of)


def remote(*dims, of=f32):
    return pltpu.HBM(dims, of)


def free(*dims, of=f32):
    return jax.ShapeDtypeStruct(dims, of)


def fetch(source, target, done):
    copy = pltpu.make_async_copy(source, target, done)
    copy.start()
    return copy


def count_tables(counts_ref, logs_ref, target_ref, weight_ref):
    for at in range(0, ROWS, TILE):
        base = logs_ref[at : at + TILE, :]
        for side in range(0, 2 * HALF, HALF):
            counts = counts_ref[at : at + TILE, side : side + HALF].astype(f32)
            target_ref[at : at + TILE, side : side + HALF] = jnp.log(jnp.maximum(counts, 1.0)) + base
            weight = loss_scale * (0.1 + 0.25 * jnp.sqrt(counts))
            weight_ref[at : at + TILE, side : side + HALF] = jnp.where(counts > 0.5, weight, 0.0)


def prep_body(
    row_hbm, counts_hbm, vecs_hbm, moment_hbm, row_sums_hbm, col_sums_hbm,
    hi_ref, lo_ref, turned_hi_ref, turned_lo_ref, logs_ref, target_ref, weight_ref, left_ref, right_ref,
    given_ref, row_ref, counts_ref, vecs_ref, moment_ref, row_sums_ref, col_sums_ref, done,
):
    get_row_sums = fetch(row_sums_hbm, row_sums_ref, done.at[4])
    get_counts = fetch(counts_hbm.at[0], counts_ref, done.at[0])
    get_rows = fetch(row_hbm, given_ref, done.at[1])
    get_vecs = fetch(vecs_hbm, vecs_ref, done.at[2])
    get_moment = fetch(moment_hbm, moment_ref, done.at[3])
    get_col_sums = fetch(col_sums_hbm, col_sums_ref, done.at[5])
    get_row_sums.wait()
    logs = log_total - jnp.log(row_sums_ref[...].astype(f32))
    logs_ref[...] = jnp.broadcast_to(logs, (HALF, ROWS)).T
    row_ref[WIDTH:, :] = jnp.zeros((LANES - WIDTH, ROWS), f32)
    get_counts.wait()
    count_tables(counts_ref, logs_ref, target_ref, weight_ref)
    get_rows.wait()
    row_ref[0:WIDTH, :] = given_ref[...]
    high, low = split(given_ref[...])
    hi_ref[...] = high
    lo_ref[...] = low
    for at in range(0, ROWS, TILE):
        high, low = split(row_ref[:, at : at + TILE].T)
        turned_hi_ref[at : at + TILE, :] = high
        turned_lo_ref[at : at + TILE, :] = low
    get_vecs.wait()
    get_moment.wait()
    get_col_sums.wait()
    for side, ref in enumerate((left_ref, right_ref)):
        lanes = slice(side * HALF, (side + 1) * HALF)
        ref[0:WIDTH, :] = vecs_ref[:, lanes]
        ref[WIDTH:PADW, :] = jnp.broadcast_to(jnp.log(col_sums_ref[:, lanes].astype(f32)), (PADW - WIDTH, HALF))
        ref[PADW : PADW + WIDTH, :] = moment_ref[:, lanes]
        ref[PADW + WIDTH :, :] = jnp.zeros((PADW - WIDTH, HALF), f32)


def shares_body(row_hbm, acc_hbm, vecs_ref, moment_ref, given_ref, block_ref, turned_ref, done):
    group = lax.axis_index("grp")
    lanes = pl.ds(pl.multiple_of((group >> 2) * 128, 128), 128)
    gets = [fetch(source.at[:, lanes], given_ref.at[at], done.at[at]) for at, source in enumerate((row_hbm, acc_hbm))]
    for at, ref in enumerate((vecs_ref, moment_ref)):
        gets[at].wait()
        block_ref[0:WIDTH, :] = given_ref[at]
        block_ref[WIDTH:, :] = jnp.zeros((LANES - WIDTH, 128), f32)
        turned_ref[...] = block_ref[...].T
        ref[...] = turned_ref[pl.ds(pl.multiple_of((group & 3) * SHARE, SHARE), SHARE), 0:WIDTH]


def split_columns(vecs, both_ref):
    inside = lax.broadcasted_iota(jnp.int32, (PADW, HALF), 0) < WIDTH
    high, low = split(jnp.where(inside, vecs, 0.0))
    both_ref[0:PADW, 0:HALF] = high
    both_ref[0:PADW, HALF:] = low
    both_ref[PADW:, :] = jnp.zeros((LANES - PADW, 2 * HALF), bf16)


def cells(col_logs, both_ref, turned_hi_ref, turned_lo_ref, target_ref, weight_ref, grad_ref, side):
    for at in range(0, ROWS, TILE):
        rows = slice(at, at + TILE)
        lanes = slice(side * HALF, (side + 1) * HALF)
        wide = dot(turned_hi_ref[rows, :], both_ref[...])
        scores = wide[:, :HALF] + wide[:, HALF:] + dot(turned_lo_ref[rows, :], both_ref[:, :HALF])
        residue = scores - (target_ref[rows, lanes] - col_logs)
        weight = weight_ref[rows, lanes]
        seen = weight * residue
        unseen = loss_scale / (1.0 + jnp.exp(-residue))
        high, low = split(jnp.where(weight > 0.0, seen, unseen))
        grad_ref[rows, :HALF] = high
        grad_ref[rows, HALF:] = low


def col_grads(hi_ref, lo_ref, grad_ref):
    wide = dot(hi_ref[...], grad_ref[...])
    return wide[:, :HALF] + wide[:, HALF:] + dot(lo_ref[...], grad_ref[:, :HALF])


def updated(vecs, moment, grad):
    new_moment = moment + grad * grad
    return vecs - step_rate * grad / jnp.sqrt(new_moment), new_moment


def first_visit_body(side, state_ref, turned_hi_ref, turned_lo_ref, hi_ref, lo_ref, target_ref, weight_ref, vecs_ref, moment_ref, grad_ref, both_ref):
    split_columns(state_ref[0:PADW, :], both_ref)
    cells(state_ref[WIDTH : WIDTH + 1, :], both_ref, turned_hi_ref, turned_lo_ref, target_ref, weight_ref, grad_ref, side)
    grad = col_grads(hi_ref, lo_ref, grad_ref)
    vecs, moment = updated(state_ref[0:WIDTH, :], state_ref[PADW : PADW + WIDTH, :], grad)
    vecs_ref[0:WIDTH, :] = vecs
    vecs_ref[WIDTH:, :] = state_ref[WIDTH:PADW, :]
    moment_ref[0:WIDTH, :] = moment
    moment_ref[WIDTH:, :] = jnp.zeros((PADW - WIDTH, HALF), f32)


def second_visit_body(side, vecs_ref, turned_hi_ref, turned_lo_ref, hi_ref, lo_ref, target_ref, weight_ref, out_ref, grad_ref, both_ref):
    split_columns(vecs_ref[...], both_ref)
    cells(vecs_ref[WIDTH : WIDTH + 1, :], both_ref, turned_hi_ref, turned_lo_ref, target_ref, weight_ref, grad_ref, side)
    out_ref[0:WIDTH, :] = col_grads(hi_ref, lo_ref, grad_ref)
    out_ref[WIDTH:, :] = jnp.zeros((PADW - WIDTH, HALF), f32)


def third_visit_body(side, whole_ref, sent_ref, turned_hi_ref, turned_lo_ref, hi_ref, lo_ref, target_ref, weight_ref, *refs):
    now_ref, vecs_ref, moment_ref, grad_ref, both_ref = refs[-5:]
    if side:
        moment_ref[0:PADW, :] = refs[0][...]
    at = side * 2 * PADW
    vecs, moment = updated(whole_ref[at : at + WIDTH, :], whole_ref[at + PADW : at + PADW + WIDTH, :], sent_ref[0:WIDTH, :])
    now_ref[0:WIDTH, :] = vecs
    now_ref[WIDTH:, :] = whole_ref[at + WIDTH : at + PADW, :]
    split_columns(now_ref[...], both_ref)
    cells(now_ref[WIDTH : WIDTH + 1, :], both_ref, turned_hi_ref, turned_lo_ref, target_ref, weight_ref, grad_ref, side)
    vecs, moment = updated(now_ref[0:WIDTH, :], moment, col_grads(hi_ref, lo_ref, grad_ref))
    vecs_ref[0:WIDTH, :] = vecs
    vecs_ref[WIDTH:, :] = now_ref[WIDTH:, :]
    moment_ref[side * PADW : side * PADW + WIDTH, :] = moment
    moment_ref[side * PADW + WIDTH : (side + 1) * PADW, :] = jnp.zeros((PADW - WIDTH, HALF), f32)


def last_update_body(kept_a_hbm, kept_b_hbm, col_grad_a_hbm, col_grad_b_hbm, moments_ref, new_ref, new_moment_ref, *scratch):
    *refs, done = scratch
    sources = (kept_a_hbm, kept_b_hbm, col_grad_a_hbm, col_grad_b_hbm)
    gets = [fetch(source, ref, done.at[at]) for at, (source, ref) in enumerate(zip(sources, refs))]
    for get in gets:
        get.wait()
    for side in range(2):
        vecs, moment = updated(refs[side][0:WIDTH, :], moments_ref[side * PADW : side * PADW + WIDTH, :], refs[2 + side][0:WIDTH, :])
        new_ref[:, side * HALF : (side + 1) * HALF] = vecs
        new_moment_ref[:, side * HALF : (side + 1) * HALF] = moment


def spread(vecs_ref, high_ref, low_ref):
    main_high, main_low = split(vecs_ref[0:256, :])
    tail = vecs_ref[256:PADW, :]
    inside = lax.broadcasted_iota(jnp.int32, (PADW - 256, HALF), 0) < WIDTH - 256
    tail_high, tail_low = split(jnp.where(inside, tail, 0.0))
    gap = jnp.zeros((64 - (PADW - 256), HALF), bf16)
    places = ((high_ref, 0, main_high, tail_high), (high_ref, HALF, main_high, tail_high), (low_ref, 0, main_low, tail_low))
    for ref, at, main, rest in places:
        ref[0:256, at : at + HALF] = main
        for start in (256, 320):
            ref[start : start + PADW - 256, at : at + HALF] = rest
            ref[start + PADW - 256 : start + 64, at : at + HALF] = gap


def row_part(grad_ref, high_ref, low_ref, rows):
    by_columns = (((1,), (1,)), ((), ()))
    part = lax.dot_general(grad_ref[rows, :], high_ref[...], by_columns, preferred_element_type=f32)
    return part + lax.dot_general(grad_ref[rows, :HALF], low_ref[...], by_columns, preferred_element_type=f32)


SPREAD = [pltpu.VMEM((LANES, 2 * HALF), bf16), pltpu.VMEM((LANES, HALF), bf16)]


def pack_body(*refs):
    for at, ref in enumerate(refs[:-1]):
        refs[-1][at * PADW : (at + 1) * PADW, :] = ref[...]


def tables_body(turn, counts_hbm, logs_ref, after_ref, target_ref, weight_ref, counts_ref, done):
    get_counts = fetch(counts_hbm.at[turn + 1], counts_ref, done)
    get_counts.wait()
    count_tables(counts_ref, logs_ref, target_ref, weight_ref)


def rows_body(more, vecs_a_ref, vecs_b_ref, grad_a_ref, grad_b_ref, *refs):
    before_ref = refs[0] if more else None
    total_ref, high_a_ref, low_a_ref, high_b_ref, low_b_ref = refs[-5:]
    spread(vecs_a_ref, high_a_ref, low_a_ref)
    spread(vecs_b_ref, high_b_ref, low_b_ref)
    for at in range(0, ROWS, TILE):
        rows = slice(at, at + TILE)
        part = row_part(grad_a_ref, high_a_ref, low_a_ref, rows) + row_part(grad_b_ref, high_b_ref, low_b_ref, rows)
        total_ref[rows, :] = before_ref[rows, :] + part if more else part


def last_half(side, vecs_ref, turned_hi_ref, turned_lo_ref, target_ref, weight_ref, before_ref, grad_ref, total_ref, both_ref, high_ref, low_ref):
    split_columns(vecs_ref[0:PADW, :], both_ref)
    cells(vecs_ref[WIDTH : WIDTH + 1, :], both_ref, turned_hi_ref, turned_lo_ref, target_ref, weight_ref, grad_ref, side)
    spread(vecs_ref, high_ref, low_ref)
    for at in range(0, ROWS, TILE):
        rows = slice(at, at + TILE)
        total_ref[rows, :] = before_ref[rows, :] + row_part(grad_ref, high_ref, low_ref, rows)


def keep_columns(vecs_ref, hi_ref, lo_ref, grad_ref, kept_ref, col_grad_ref):
    kept_ref[...] = vecs_ref[...]
    col_grad_ref[0:WIDTH, :] = col_grads(hi_ref, lo_ref, grad_ref)
    col_grad_ref[WIDTH:, :] = jnp.zeros((PADW - WIDTH, HALF), f32)


def last_first_body(vecs_ref, turned_hi_ref, turned_lo_ref, target_ref, weight_ref, before_ref, hi_ref, lo_ref, total_ref, kept_ref, col_grad_ref, grad_ref, *scratch):
    last_half(0, vecs_ref, turned_hi_ref, turned_lo_ref, target_ref, weight_ref, before_ref, grad_ref, total_ref, *scratch)
    keep_columns(vecs_ref, hi_ref, lo_ref, grad_ref, kept_ref, col_grad_ref)


def last_body(side, vecs_ref, turned_hi_ref, turned_lo_ref, target_ref, weight_ref, before_ref, grad_ref, keep_ref, send_ref, total_ref, *scratch):
    last_half(side, vecs_ref, turned_hi_ref, turned_lo_ref, target_ref, weight_ref, before_ref, grad_ref, total_ref, *scratch)
    core = lax.axis_index("grp") & 1
    left = lax.broadcasted_iota(jnp.int32, (8, 128), 1) < 64
    for ref, half in ((keep_ref, core), (send_ref, 1 - core)):
        for slot in range(16):
            base = pl.multiple_of(slot * 2 * SHARE + half * SHARE, SHARE)
            block = total_ref[pl.ds(base, SHARE), :]
            ref[slot * PACK : slot * PACK + SHARE, :] = block[:, :256]
            for pair in range(2):
                upper = block[pair * 16 : pair * 16 + 8, 256:]
                lower = block[pair * 16 + 8 : pair * 16 + 16, 256:]
                ref[slot * PACK + SHARE : (slot + 1) * PACK, pair * 128 : (pair + 1) * 128] = jnp.where(left, upper, lower)


def sum_body(kept_ref, moments_ref, keep_ref, got_ref, out_ref):
    for slot in range(16):
        rows = slice(slot * PACK, (slot + 1) * PACK)
        out_ref[slot] = keep_ref[rows, :] + got_ref[rows, :]


def finish_body(parts_ref, vecs_ref, moment_ref, new_ref, new_moment_ref, grad_ref):
    total = parts_ref[0]
    for at in range(1, parts_ref.shape[0]):
        total = total + parts_ref[at]
    grad_ref[:, :256] = total[0:SHARE, :]
    for group in range(4):
        rest = total[SHARE:PACK, (group // 2) * 128 : (group // 2 + 1) * 128]
        if group % 2:
            rest = pltpu.roll(rest, 64, 1)
        grad_ref[group * 8 : (group + 1) * 8, 256:] = rest
    vecs, moment = updated(vecs_ref[...], moment_ref[...], grad_ref[:, :WIDTH])
    new_ref[...] = vecs
    new_moment_ref[...] = moment


def shifted(value, steps=1):
    count = lax.axis_size("blk")
    return lax.ppermute(value, "blk", [(source, (source + steps) % count) for source in range(count)])


def swapped(value, bit):
    count = lax.axis_size("grp")
    return lax.ppermute(value, "grp", [(source, source ^ bit) for source in range(count)])


def shards(counts, row_sums, col_sums, row_emb, row_acc, col_emb, col_acc):
    cell_half = near(ROWS, 2 * HALF, of=bf16)
    table = near(ROWS, 2 * HALF)
    both = pltpu.VMEM((LANES, 2 * HALF), bf16)

    hi, lo, turned_hi, turned_lo, row_logs, target, weight, *states = call(
        "prep",
        prep_body,
        (near(WIDTH, ROWS, of=bf16),) * 2 + (near(ROWS, LANES, of=bf16),) * 2 + (near(ROWS, HALF), table, table) + (near(2 * PADW, HALF),) * 2,
        (row_emb, counts, col_emb, col_acc, row_sums.reshape(1, ROWS), col_sums.reshape(1, 2 * HALF)),
        [
            pltpu.VMEM((WIDTH, ROWS), f32),
            pltpu.VMEM((LANES, ROWS), f32),
            pltpu.VMEM((ROWS, 2 * HALF), bf16),
            pltpu.VMEM((WIDTH, 2 * HALF), f32),
            pltpu.VMEM((WIDTH, 2 * HALF), f32),
            pltpu.VMEM((1, ROWS), jnp.int32),
            pltpu.VMEM((1, 2 * HALF), jnp.int32),
            pltpu.SemaphoreType.DMA((6,)),
        ],
        far=6,
        room=6,
    )

    rows = (turned_hi, turned_lo, hi, lo)

    def beside(turn, vecs, grads, after, *more):
        target, weight = call(
            "tables",
            lambda *refs: tables_body(turn, *refs),
            (table, table),
            (counts, row_logs, after),
            [pltpu.VMEM((ROWS, 2 * HALF), bf16), pltpu.SemaphoreType.DMA(())],
            far=1,
            flops=1 << 20,
        )
        total = call(
            "rows",
            lambda *refs: rows_body(turn > 0, *refs),
            near(ROWS, LANES),
            (*vecs, *grads, *more),
            SPREAD * 2,
            flops=1 << 20,
        )
        return total, target, weight

    near_vecs = near(PADW, HALF)
    vecs, moments, grads = [None] * 2, [None] * 2, [None] * 2
    for side in range(2):
        vecs[side], moments[side], grads[side] = call(
            "first_visit",
            lambda *refs, side=side: first_visit_body(side, *refs),
            (near_vecs, near_vecs, cell_half),
            (states[side], *rows, target, weight),
            [both],
        )
    whole = call("pack", pack_body, near(4 * PADW, HALF), (vecs[0], moments[0], vecs[1], moments[1]), flops=1 << 20)
    total, target, weight = beside(0, states, grads, whole)
    whole = shifted(whole, 2)
    vecs = [shifted(each) for each in vecs]

    sent, grads = [None] * 2, [None] * 2
    for side in range(2):
        sent[side], grads[side] = call(
            "second_visit",
            lambda *refs, side=side: second_visit_body(side, *refs),
            (near_vecs, cell_half),
            (vecs[side], *rows, target, weight),
            [both],
        )
        sent[side] = shifted(sent[side])
    total, target, weight = beside(1, vecs, grads, grads[1], total)

    now, vecs, grads, moments = [None] * 2, [None] * 2, [None] * 2, ()
    for side in range(2):
        now[side], vecs[side], *moments, grads[side] = call(
            "third_visit",
            lambda *refs, side=side: third_visit_body(side, *refs),
            (near_vecs, near_vecs, near((1 + side) * PADW, HALF), cell_half),
            (whole, sent[side], *rows, target, weight, *moments),
            [both],
        )
        vecs[side] = shifted(vecs[side])
    moments = shifted(moments[0])
    total, target, weight = beside(2, now, grads, grads[1], total)

    part, kept_a, col_grad_a = call(
        "last_first",
        last_first_body,
        (near(ROWS, LANES), remote(PADW, HALF), remote(PADW, HALF)),
        (vecs[0], turned_hi, turned_lo, target, weight, total, hi, lo),
        [pltpu.VMEM((ROWS, 2 * HALF), bf16), both] + SPREAD,
    )
    grad_b, keep, send = call(
        "last_second",
        lambda *refs: last_body(1, *refs),
        (cell_half, near(16 * PACK, 256), near(16 * PACK, 256)),
        (vecs[1], turned_hi, turned_lo, target, weight, part),
        [pltpu.VMEM((ROWS, LANES), f32), both] + SPREAD,
        room=6,
    )
    kept_b, col_grad_b = call(
        "last_columns",
        keep_columns,
        (remote(PADW, HALF), remote(PADW, HALF)),
        (vecs[1], hi, lo, grad_b),
        flops=1 << 33,
    )
    small = pltpu.VMEM((PADW, HALF), f32)
    new_col_emb, new_col_acc = call(
        "last_update",
        last_update_body,
        (free(WIDTH, 2 * HALF), free(WIDTH, 2 * HALF)),
        (kept_a, kept_b, col_grad_a, col_grad_b, moments),
        [small] * 4 + [pltpu.SemaphoreType.DMA((4,))],
        far=4,
        flops=1 << 20,
    )

    own_vecs, own_moment = call(
        "shares",
        shares_body,
        (near(SHARE, WIDTH), near(SHARE, WIDTH)),
        (row_emb, row_acc),
        [pltpu.VMEM((2, WIDTH, 128), f32), pltpu.VMEM((LANES, 128), f32), pltpu.VMEM((128, LANES), f32), pltpu.SemaphoreType.DMA((2,))],
        far=2,
    )
    got = swapped(send, 1)
    share = call("sum", sum_body, near(16, PACK, 256), (kept_b, moments, keep, got), far=1)
    chips = [[2 * chip + core for chip in range(16)] for core in range(2)]
    parts = lax.all_to_all(share, "grp", 0, 0, axis_index_groups=chips)

    new_rows, new_row_moment = call(
        "finish",
        finish_body,
        (free(SHARE, WIDTH), free(SHARE, WIDTH)),
        (parts, own_vecs, own_moment),
        [pltpu.VMEM((SHARE, LANES), f32)],
    )
    return (new_rows.T, new_row_moment.T, new_col_emb, new_col_acc)


def solution(mesh):
    return jax.shard_map(
        shards,
        mesh=mesh,
        in_specs=(
            P(None, "blk", "grp"),
            P("blk"),
            P(("blk", "grp")),
            P(None, "blk"),
            P(None, "blk"),
            P(None, ("blk", "grp")),
            P(None, ("blk", "grp")),
        ),
        out_specs=(
            P(None, ("blk", "grp")),
            P(None, ("blk", "grp")),
            P(None, ("blk", "grp")),
            P(None, ("blk", "grp")),
        ),
        check_vma=False,
    )
```

```python
import jax
import jax.numpy as jnp
from jax import lax
from jax.experimental import pallas as pl
from jax.experimental.pallas import tpu as pltpu
from jax.sharding import PartitionSpec as P

log_total = 20.0
loss_scale = 1.0 / 256.0
step_rate = 0.1

WIDTH = 300
PADW = 304
LANES = 384
ROWS = 1024
HALF = 128
TILE = 256
SHARE = 32
PACK = 40

f32 = jnp.float32
bf16 = jnp.bfloat16
VM = pl.BlockSpec(memory_space=pltpu.VMEM)
FAR = pl.BlockSpec(memory_space=pl.ANY)


def split(value):
    high = value.astype(bf16)
    return high, (value - high.astype(f32)).astype(bf16)


def dot(left, right):
    return jnp.dot(left, right, preferred_element_type=f32)


def call(name, body, out, operands, scratch=(), far=0, room=4, flops=1 << 32):
    specs = [FAR] * far + [VM] * (len(operands) - far)
    spaces = [pltpu.HBM] * far + [pltpu.VMEM] * (len(operands) - far)
    placed = [pltpu.with_memory_space_constraint(each, space) for each, space in zip(operands, spaces)]
    return pl.pallas_call(
        body,
        out_shape=out,
        in_specs=specs,
        out_specs=jax.tree.map(lambda _: VM, out),
        scratch_shapes=list(scratch),
        compiler_params=pltpu.CompilerParams(vmem_limit_bytes=room * 1024 * 1024),
        cost_estimate=pl.CostEstimate(flops=flops, bytes_accessed=1 << 10, transcendentals=0),
        name=name,
    )(*placed)


def near(*dims, of=f32):
    return pltpu.VMEM(dims, of)


def remote(*dims, of=f32):
    return pltpu.HBM(dims, of)


def free(*dims, of=f32):
    return jax.ShapeDtypeStruct(dims, of)


def fetch(source, target, done):
    copy = pltpu.make_async_copy(source, target, done)
    copy.start()
    return copy


def count_tables(counts_ref, logs_ref, target_ref, weight_ref):
    for at in range(0, ROWS, TILE):
        base = logs_ref[at : at + TILE, :]
        for side in range(0, 2 * HALF, HALF):
            counts = counts_ref[at : at + TILE, side : side + HALF].astype(f32)
            target_ref[at : at + TILE, side : side + HALF] = jnp.log(jnp.maximum(counts, 1.0)) + base
            weight = loss_scale * (0.1 + 0.25 * jnp.sqrt(counts))
            weight_ref[at : at + TILE, side : side + HALF] = jnp.where(counts > 0.5, weight, 0.0)


def prep_body(
    row_hbm, counts_hbm, vecs_hbm, moment_hbm, row_sums_hbm, col_sums_hbm,
    hi_ref, lo_ref, turned_hi_ref, turned_lo_ref, logs_ref, target_ref, weight_ref, left_ref, right_ref,
    given_ref, row_ref, counts_ref, vecs_ref, moment_ref, row_sums_ref, col_sums_ref, done,
):
    get_row_sums = fetch(row_sums_hbm, row_sums_ref, done.at[4])
    get_counts = fetch(counts_hbm.at[0], counts_ref, done.at[0])
    get_rows = fetch(row_hbm, given_ref, done.at[1])
    get_vecs = fetch(vecs_hbm, vecs_ref, done.at[2])
    get_moment = fetch(moment_hbm, moment_ref, done.at[3])
    get_col_sums = fetch(col_sums_hbm, col_sums_ref, done.at[5])
    get_row_sums.wait()
    logs = log_total - jnp.log(row_sums_ref[...].astype(f32))
    logs_ref[...] = jnp.broadcast_to(logs, (HALF, ROWS)).T
    row_ref[WIDTH:, :] = jnp.zeros((LANES - WIDTH, ROWS), f32)
    get_counts.wait()
    count_tables(counts_ref, logs_ref, target_ref, weight_ref)
    get_rows.wait()
    row_ref[0:WIDTH, :] = given_ref[...]
    high, low = split(given_ref[...])
    hi_ref[...] = high
    lo_ref[...] = low
    for at in range(0, ROWS, TILE):
        high, low = split(row_ref[:, at : at + TILE].T)
        turned_hi_ref[at : at + TILE, :] = high
        turned_lo_ref[at : at + TILE, :] = low
    get_vecs.wait()
    get_moment.wait()
    get_col_sums.wait()
    for side, ref in enumerate((left_ref, right_ref)):
        lanes = slice(side * HALF, (side + 1) * HALF)
        ref[0:WIDTH, :] = vecs_ref[:, lanes]
        ref[WIDTH:PADW, :] = jnp.broadcast_to(jnp.log(col_sums_ref[:, lanes].astype(f32)), (PADW - WIDTH, HALF))
        ref[PADW : PADW + WIDTH, :] = moment_ref[:, lanes]
        ref[PADW + WIDTH :, :] = jnp.zeros((PADW - WIDTH, HALF), f32)


def shares_body(row_hbm, acc_hbm, vecs_ref, moment_ref, given_ref, block_ref, turned_ref, done):
    group = lax.axis_index("grp")
    lanes = pl.ds(pl.multiple_of((group >> 2) * 128, 128), 128)
    gets = [fetch(source.at[:, lanes], given_ref.at[at], done.at[at]) for at, source in enumerate((row_hbm, acc_hbm))]
    for at, ref in enumerate((vecs_ref, moment_ref)):
        gets[at].wait()
        block_ref[0:WIDTH, :] = given_ref[at]
        block_ref[WIDTH:, :] = jnp.zeros((LANES - WIDTH, 128), f32)
        turned_ref[...] = block_ref[...].T
        ref[...] = turned_ref[pl.ds(pl.multiple_of((group & 3) * SHARE, SHARE), SHARE), 0:WIDTH]


def split_columns(vecs, both_ref):
    inside = lax.broadcasted_iota(jnp.int32, (PADW, HALF), 0) < WIDTH
    high, low = split(jnp.where(inside, vecs, 0.0))
    both_ref[0:PADW, 0:HALF] = high
    both_ref[0:PADW, HALF:] = low
    both_ref[PADW:, :] = jnp.zeros((LANES - PADW, 2 * HALF), bf16)


def cells(col_logs, both_ref, turned_hi_ref, turned_lo_ref, target_ref, weight_ref, grad_ref, side):
    for at in range(0, ROWS, TILE):
        rows = slice(at, at + TILE)
        lanes = slice(side * HALF, (side + 1) * HALF)
        wide = dot(turned_hi_ref[rows, :], both_ref[...])
        scores = wide[:, :HALF] + wide[:, HALF:] + dot(turned_lo_ref[rows, :], both_ref[:, :HALF])
        residue = scores - (target_ref[rows, lanes] - col_logs)
        weight = weight_ref[rows, lanes]
        seen = weight * residue
        unseen = loss_scale / (1.0 + jnp.exp(-residue))
        high, low = split(jnp.where(weight > 0.0, seen, unseen))
        grad_ref[rows, :HALF] = high
        grad_ref[rows, HALF:] = low


def col_grads(hi_ref, lo_ref, grad_ref):
    wide = dot(hi_ref[...], grad_ref[...])
    return wide[:, :HALF] + wide[:, HALF:] + dot(lo_ref[...], grad_ref[:, :HALF])


def updated(vecs, moment, grad):
    new_moment = moment + grad * grad
    return vecs - step_rate * grad / jnp.sqrt(new_moment), new_moment


def first_visit_body(side, state_ref, turned_hi_ref, turned_lo_ref, hi_ref, lo_ref, target_ref, weight_ref, vecs_ref, moment_ref, grad_ref, both_ref):
    split_columns(state_ref[0:PADW, :], both_ref)
    cells(state_ref[WIDTH : WIDTH + 1, :], both_ref, turned_hi_ref, turned_lo_ref, target_ref, weight_ref, grad_ref, side)
    grad = col_grads(hi_ref, lo_ref, grad_ref)
    vecs, moment = updated(state_ref[0:WIDTH, :], state_ref[PADW : PADW + WIDTH, :], grad)
    vecs_ref[0:WIDTH, :] = vecs
    vecs_ref[WIDTH:, :] = state_ref[WIDTH:PADW, :]
    moment_ref[0:WIDTH, :] = moment
    moment_ref[WIDTH:, :] = jnp.zeros((PADW - WIDTH, HALF), f32)


def second_visit_body(side, vecs_ref, turned_hi_ref, turned_lo_ref, hi_ref, lo_ref, target_ref, weight_ref, out_ref, grad_ref, both_ref):
    split_columns(vecs_ref[...], both_ref)
    cells(vecs_ref[WIDTH : WIDTH + 1, :], both_ref, turned_hi_ref, turned_lo_ref, target_ref, weight_ref, grad_ref, side)
    out_ref[0:WIDTH, :] = col_grads(hi_ref, lo_ref, grad_ref)
    out_ref[WIDTH:, :] = jnp.zeros((PADW - WIDTH, HALF), f32)


def third_visit_body(side, whole_ref, sent_ref, turned_hi_ref, turned_lo_ref, hi_ref, lo_ref, target_ref, weight_ref, *refs):
    now_ref, vecs_ref, moment_ref, grad_ref, both_ref = refs[-5:]
    if side:
        moment_ref[0:PADW, :] = refs[0][...]
    at = side * 2 * PADW
    vecs, moment = updated(whole_ref[at : at + WIDTH, :], whole_ref[at + PADW : at + PADW + WIDTH, :], sent_ref[0:WIDTH, :])
    now_ref[0:WIDTH, :] = vecs
    now_ref[WIDTH:, :] = whole_ref[at + WIDTH : at + PADW, :]
    split_columns(now_ref[...], both_ref)
    cells(now_ref[WIDTH : WIDTH + 1, :], both_ref, turned_hi_ref, turned_lo_ref, target_ref, weight_ref, grad_ref, side)
    vecs, moment = updated(now_ref[0:WIDTH, :], moment, col_grads(hi_ref, lo_ref, grad_ref))
    vecs_ref[0:WIDTH, :] = vecs
    vecs_ref[WIDTH:, :] = now_ref[WIDTH:, :]
    moment_ref[side * PADW : side * PADW + WIDTH, :] = moment
    moment_ref[side * PADW + WIDTH : (side + 1) * PADW, :] = jnp.zeros((PADW - WIDTH, HALF), f32)


def last_update_body(kept_a_hbm, kept_b_hbm, col_grad_a_hbm, col_grad_b_hbm, moments_ref, new_ref, new_moment_ref, *scratch):
    *refs, done = scratch
    sources = (kept_a_hbm, kept_b_hbm, col_grad_a_hbm, col_grad_b_hbm)
    gets = [fetch(source, ref, done.at[at]) for at, (source, ref) in enumerate(zip(sources, refs))]
    for get in gets:
        get.wait()
    for side in range(2):
        vecs, moment = updated(refs[side][0:WIDTH, :], moments_ref[side * PADW : side * PADW + WIDTH, :], refs[2 + side][0:WIDTH, :])
        new_ref[:, side * HALF : (side + 1) * HALF] = vecs
        new_moment_ref[:, side * HALF : (side + 1) * HALF] = moment


def spread(vecs_ref, high_ref, low_ref):
    main_high, main_low = split(vecs_ref[0:256, :])
    tail = vecs_ref[256:PADW, :]
    inside = lax.broadcasted_iota(jnp.int32, (PADW - 256, HALF), 0) < WIDTH - 256
    tail_high, tail_low = split(jnp.where(inside, tail, 0.0))
    gap = jnp.zeros((64 - (PADW - 256), HALF), bf16)
    places = ((high_ref, 0, main_high, tail_high), (high_ref, HALF, main_high, tail_high), (low_ref, 0, main_low, tail_low))
    for ref, at, main, rest in places:
        ref[0:256, at : at + HALF] = main
        for start in (256, 320):
            ref[start : start + PADW - 256, at : at + HALF] = rest
            ref[start + PADW - 256 : start + 64, at : at + HALF] = gap


def row_part(grad_ref, high_ref, low_ref, rows):
    by_columns = (((1,), (1,)), ((), ()))
    part = lax.dot_general(grad_ref[rows, :], high_ref[...], by_columns, preferred_element_type=f32)
    return part + lax.dot_general(grad_ref[rows, :HALF], low_ref[...], by_columns, preferred_element_type=f32)


SPREAD = [pltpu.VMEM((LANES, 2 * HALF), bf16), pltpu.VMEM((LANES, HALF), bf16)]


def pack_body(*refs):
    for at, ref in enumerate(refs[:-1]):
        refs[-1][at * PADW : (at + 1) * PADW, :] = ref[...]


def tables_body(turn, counts_hbm, logs_ref, after_ref, target_ref, weight_ref, counts_ref, done):
    get_counts = fetch(counts_hbm.at[turn + 1], counts_ref, done)
    get_counts.wait()
    count_tables(counts_ref, logs_ref, target_ref, weight_ref)


def rows_body(more, vecs_a_ref, vecs_b_ref, grad_a_ref, grad_b_ref, *refs):
    before_ref = refs[0] if more else None
    total_ref, high_a_ref, low_a_ref, high_b_ref, low_b_ref = refs[-5:]
    spread(vecs_a_ref, high_a_ref, low_a_ref)
    spread(vecs_b_ref, high_b_ref, low_b_ref)
    for at in range(0, ROWS, TILE):
        rows = slice(at, at + TILE)
        part = row_part(grad_a_ref, high_a_ref, low_a_ref, rows) + row_part(grad_b_ref, high_b_ref, low_b_ref, rows)
        total_ref[rows, :] = before_ref[rows, :] + part if more else part


def last_half(side, vecs_ref, turned_hi_ref, turned_lo_ref, target_ref, weight_ref, before_ref, grad_ref, total_ref, both_ref, high_ref, low_ref):
    split_columns(vecs_ref[0:PADW, :], both_ref)
    cells(vecs_ref[WIDTH : WIDTH + 1, :], both_ref, turned_hi_ref, turned_lo_ref, target_ref, weight_ref, grad_ref, side)
    spread(vecs_ref, high_ref, low_ref)
    for at in range(0, ROWS, TILE):
        rows = slice(at, at + TILE)
        total_ref[rows, :] = before_ref[rows, :] + row_part(grad_ref, high_ref, low_ref, rows)


def keep_columns(vecs_ref, hi_ref, lo_ref, grad_ref, kept_ref, col_grad_ref):
    kept_ref[...] = vecs_ref[...]
    col_grad_ref[0:WIDTH, :] = col_grads(hi_ref, lo_ref, grad_ref)
    col_grad_ref[WIDTH:, :] = jnp.zeros((PADW - WIDTH, HALF), f32)


def last_first_body(vecs_ref, turned_hi_ref, turned_lo_ref, target_ref, weight_ref, before_ref, hi_ref, lo_ref, total_ref, kept_ref, col_grad_ref, grad_ref, *scratch):
    last_half(0, vecs_ref, turned_hi_ref, turned_lo_ref, target_ref, weight_ref, before_ref, grad_ref, total_ref, *scratch)
    keep_columns(vecs_ref, hi_ref, lo_ref, grad_ref, kept_ref, col_grad_ref)


def last_body(side, vecs_ref, turned_hi_ref, turned_lo_ref, target_ref, weight_ref, before_ref, grad_ref, keep_ref, send_ref, total_ref, *scratch):
    last_half(side, vecs_ref, turned_hi_ref, turned_lo_ref, target_ref, weight_ref, before_ref, grad_ref, total_ref, *scratch)
    core = lax.axis_index("grp") & 1
    left = lax.broadcasted_iota(jnp.int32, (8, 128), 1) < 64
    for ref, half in ((keep_ref, core), (send_ref, 1 - core)):
        for slot in range(16):
            base = pl.multiple_of(slot * 2 * SHARE + half * SHARE, SHARE)
            block = total_ref[pl.ds(base, SHARE), :]
            ref[slot * PACK : slot * PACK + SHARE, :] = block[:, :256]
            for pair in range(2):
                upper = block[pair * 16 : pair * 16 + 8, 256:]
                lower = block[pair * 16 + 8 : pair * 16 + 16, 256:]
                ref[slot * PACK + SHARE : (slot + 1) * PACK, pair * 128 : (pair + 1) * 128] = jnp.where(left, upper, lower)


def sum_body(kept_ref, keep_ref, got_ref, out_ref):
    for slot in range(16):
        rows = slice(slot * PACK, (slot + 1) * PACK)
        out_ref[2 * (slot >> 3) + (slot & 1), (slot >> 1) & 3] = keep_ref[rows, :] + got_ref[rows, :]


def four_body(parts_ref, out_ref):
    for at in range(4):
        out_ref[at] = (parts_ref[0, at] + parts_ref[1, at]) + (parts_ref[2, at] + parts_ref[3, at])


def finish_body(parts_ref, vecs_ref, moment_ref, new_ref, new_moment_ref, grad_ref):
    total = parts_ref[0]
    for at in range(1, parts_ref.shape[0]):
        total = total + parts_ref[at]
    grad_ref[:, :256] = total[0:SHARE, :]
    for group in range(4):
        rest = total[SHARE:PACK, (group // 2) * 128 : (group // 2 + 1) * 128]
        if group % 2:
            rest = pltpu.roll(rest, 64, 1)
        grad_ref[group * 8 : (group + 1) * 8, 256:] = rest
    vecs, moment = updated(vecs_ref[...], moment_ref[...], grad_ref[:, :WIDTH])
    new_ref[...] = vecs
    new_moment_ref[...] = moment


def shifted(value, steps=1):
    count = lax.axis_size("blk")
    return lax.ppermute(value, "blk", [(source, (source + steps) % count) for source in range(count)])


def swapped(value, bit):
    count = lax.axis_size("grp")
    return lax.ppermute(value, "grp", [(source, source ^ bit) for source in range(count)])


def shards(counts, row_sums, col_sums, row_emb, row_acc, col_emb, col_acc):
    cell_half = near(ROWS, 2 * HALF, of=bf16)
    table = near(ROWS, 2 * HALF)
    both = pltpu.VMEM((LANES, 2 * HALF), bf16)

    hi, lo, turned_hi, turned_lo, row_logs, target, weight, *states = call(
        "prep",
        prep_body,
        (near(WIDTH, ROWS, of=bf16),) * 2 + (near(ROWS, LANES, of=bf16),) * 2 + (near(ROWS, HALF), table, table) + (near(2 * PADW, HALF),) * 2,
        (row_emb, counts, col_emb, col_acc, row_sums.reshape(1, ROWS), col_sums.reshape(1, 2 * HALF)),
        [
            pltpu.VMEM((WIDTH, ROWS), f32),
            pltpu.VMEM((LANES, ROWS), f32),
            pltpu.VMEM((ROWS, 2 * HALF), bf16),
            pltpu.VMEM((WIDTH, 2 * HALF), f32),
            pltpu.VMEM((WIDTH, 2 * HALF), f32),
            pltpu.VMEM((1, ROWS), jnp.int32),
            pltpu.VMEM((1, 2 * HALF), jnp.int32),
            pltpu.SemaphoreType.DMA((6,)),
        ],
        far=6,
        room=6,
    )

    rows = (turned_hi, turned_lo, hi, lo)

    def beside(turn, vecs, grads, after, *more):
        target, weight = call(
            "tables",
            lambda *refs: tables_body(turn, *refs),
            (table, table),
            (counts, row_logs, after),
            [pltpu.VMEM((ROWS, 2 * HALF), bf16), pltpu.SemaphoreType.DMA(())],
            far=1,
            flops=1 << 20,
        )
        total = call(
            "rows",
            lambda *refs: rows_body(turn > 0, *refs),
            near(ROWS, LANES),
            (*vecs, *grads, *more),
            SPREAD * 2,
            flops=1 << 20,
        )
        return total, target, weight

    near_vecs = near(PADW, HALF)
    vecs, moments, grads = [None] * 2, [None] * 2, [None] * 2
    for side in range(2):
        vecs[side], moments[side], grads[side] = call(
            "first_visit",
            lambda *refs, side=side: first_visit_body(side, *refs),
            (near_vecs, near_vecs, cell_half),
            (states[side], *rows, target, weight),
            [both],
        )
    whole = call("pack", pack_body, near(4 * PADW, HALF), (vecs[0], moments[0], vecs[1], moments[1]), flops=1 << 20)
    total, target, weight = beside(0, states, grads, whole)
    whole = shifted(whole, 2)
    vecs = [shifted(each) for each in vecs]

    sent, grads = [None] * 2, [None] * 2
    for side in range(2):
        sent[side], grads[side] = call(
            "second_visit",
            lambda *refs, side=side: second_visit_body(side, *refs),
            (near_vecs, cell_half),
            (vecs[side], *rows, target, weight),
            [both],
        )
        sent[side] = shifted(sent[side])
    total, target, weight = beside(1, vecs, grads, grads[1], total)

    now, vecs, grads, moments = [None] * 2, [None] * 2, [None] * 2, ()
    for side in range(2):
        now[side], vecs[side], *moments, grads[side] = call(
            "third_visit",
            lambda *refs, side=side: third_visit_body(side, *refs),
            (near_vecs, near_vecs, near((1 + side) * PADW, HALF), cell_half),
            (whole, sent[side], *rows, target, weight, *moments),
            [both],
        )
        vecs[side] = shifted(vecs[side])
    moments = shifted(moments[0])
    total, target, weight = beside(2, now, grads, grads[1], total)

    part, kept_a, col_grad_a = call(
        "last_first",
        last_first_body,
        (near(ROWS, LANES), remote(PADW, HALF), remote(PADW, HALF)),
        (vecs[0], turned_hi, turned_lo, target, weight, total, hi, lo),
        [pltpu.VMEM((ROWS, 2 * HALF), bf16), both] + SPREAD,
    )
    grad_b, keep, send = call(
        "last_second",
        lambda *refs: last_body(1, *refs),
        (cell_half, near(16 * PACK, 256), near(16 * PACK, 256)),
        (vecs[1], turned_hi, turned_lo, target, weight, part),
        [pltpu.VMEM((ROWS, LANES), f32), both] + SPREAD,
        room=6,
    )
    kept_b, col_grad_b = call(
        "last_columns",
        keep_columns,
        (remote(PADW, HALF), remote(PADW, HALF)),
        (vecs[1], hi, lo, grad_b),
        flops=1 << 20,
    )
    small = pltpu.VMEM((PADW, HALF), f32)
    new_col_emb, new_col_acc = call(
        "last_update",
        last_update_body,
        (free(WIDTH, 2 * HALF), free(WIDTH, 2 * HALF)),
        (kept_a, kept_b, col_grad_a, col_grad_b, moments),
        [small] * 4 + [pltpu.SemaphoreType.DMA((4,))],
        far=4,
        flops=1 << 20,
    )

    own_vecs, own_moment = call(
        "shares",
        shares_body,
        (near(SHARE, WIDTH), near(SHARE, WIDTH)),
        (row_emb, row_acc),
        [pltpu.VMEM((2, WIDTH, 128), f32), pltpu.VMEM((LANES, 128), f32), pltpu.VMEM((128, LANES), f32), pltpu.SemaphoreType.DMA((2,))],
        far=2,
    )
    got = swapped(send, 1)
    share = call("sum", sum_body, near(4, 4, PACK, 256), (kept_b, keep, got), far=1)
    spots = [(along_x, low, high, core) for along_x in range(2) for low in range(2) for high in range(4) for core in range(2)]
    number = {spot: spot[0] * 16 + spot[2] * 4 + spot[1] * 2 + spot[3] for spot in spots}
    squares = [[number[x, low, high, core] for x in range(2) for low in range(2)] for high in range(4) for core in range(2)]
    lines = [[number[x, low, high, core] for high in range(4)] for x in range(2) for low in range(2) for core in range(2)]
    share = lax.all_to_all(share, "grp", 0, 0, axis_index_groups=squares)
    share = call("four", four_body, near(4, PACK, 256), (share,))
    parts = lax.all_to_all(share, "grp", 0, 0, axis_index_groups=lines)

    new_rows, new_row_moment = call(
        "finish",
        finish_body,
        (free(SHARE, WIDTH), free(SHARE, WIDTH)),
        (parts, own_vecs, own_moment),
        [pltpu.VMEM((SHARE, LANES), f32)],
    )
    return (new_rows.T, new_row_moment.T, new_col_emb, new_col_acc)


def solution(mesh):
    return jax.shard_map(
        shards,
        mesh=mesh,
        in_specs=(
            P(None, "blk", "grp"),
            P("blk"),
            P(("blk", "grp")),
            P(None, "blk"),
            P(None, "blk"),
            P(None, ("blk", "grp")),
            P(None, ("blk", "grp")),
        ),
        out_specs=(
            P(None, ("blk", "grp")),
            P(None, ("blk", "grp")),
            P(None, ("blk", "grp")),
            P(None, ("blk", "grp")),
        ),
        check_vma=False,
    )
```
